32 devices in a mesh: rep: 16 (over z, y, x), tp: 2 (over core).
Axes of the slice: x: 2, y: 2, z: 4, core: 2. Of those that a mesh axis runs over, the one named last changes fastest.
Arguments:
- lookup_vectors: bfloat16 [4, 64, 128, 128], P(None, 'rep', 'tp'), may hold values from -5 to 5
- fresh_token_memory: bfloat16 [4, 64, 2, 8, 128], P(None, 'rep', None, 'tp'), may hold values from -5 to 5
- unfinished_block_memory: bfloat16 [64, 2, 16, 8, 128], P('rep', None, None, 'tp'), may hold values from -5 to 5
- cache_block_store: bfloat16 [1024, 2, 16, 8, 128], P('rep', None, None, 'tp'), may hold values from -7.5 to 7.5
- sequence_block_index: int32 [64, 128], P('rep'), may hold values from 0 to 191
- sequence_history_count: int32 [64], P('rep'), may hold values from 1 to 2048, as said below
- unfinished_block_fill: int32 [64], P('rep'), may hold values from 0 to 12
- migration_sender_block: int32 [1024], P('rep'), may hold values from 0 to 67
- migration_receiver_server: int32 [1024, 1], P('rep'), may hold values from 0 to 15; in each aligned block of 64 rows (0 to 63, 64 to 127, ...) at most 8 rows name the same one
- switch_moment: int32 [64], P('rep'), may hold values from 0 to 4
- output_scaling_weights: float32 [16384], P('tp'), may hold values from 0.5 to 1.5
Outputs:
- normed: bfloat16 [4, 64, 16384], P(None, 'rep', 'tp')
The draws below stay inside these ranges and needn't reach their ends.
Inputs may be any that keep to these rules, and one draw needn't show every extreme that they name: `sequence_block_index`: an entry below 64 names a page of the request's own replica, an entry 64 + j its arrival slot j. `sequence_history_count`: some request holds the full 128 * 16 tokens in every draw. `migration_sender_block`: an entry below 64 names a page of the replica's own pool, an entry 64 + i the tail page of its request i. `migration_receiver_server`: among the 64 entries of one replica no destination appears more than 8 times.
All inputs are finite; a program needn't handle non-finite values.
Results may differ from the reference program's by a relative error of at most 0.0056.
Values may be sent and summed in bfloat16 or wider, within the bound.
A program may use at most 64 MiB of HBM per device.

```python
import math
import jax
import jax.numpy as jnp
import numpy as np
from jax import lax

H = 128
KVH = 8
HD = 128
PAGE_TOKENS = 16
DECODE_STEP_COUNT = 4
REQ_DEV = 4
PAGES_REQ = 128
POOL_PAGE_COUNT = 64
MIG_DEV = 64
REQS = 64
PAGES_ALL = 1024
MIGS = 1024
CAP = 8
ARRIVE = 128
N_REP = 16


def draw_lookup_vectors(key, part):
    key = jax.random.fold_in(key, 11)
    first = jax.random.fold_in(key, 0)
    shape = (DECODE_STEP_COUNT, REQS, H, HD)
    base = jnp.clip(jax.random.normal(first, shape, jnp.float32), -5.0, 5.0)
    return base.astype(jnp.bfloat16)


def draw_cache_block_store(key, part):
    key = jax.random.fold_in(key, 23)
    first = jax.random.fold_in(key, 0)
    fourth = jax.random.fold_in(key, 3)
    shape = (PAGES_ALL, PAGE_TOKENS, KVH, HD)
    level = jnp.arange(KVH, dtype=jnp.float32)[None, None, :, None] / (KVH - 1)
    keys = jnp.clip(jax.random.normal(first, shape, jnp.float32), -5.0, 5.0)
    values = jnp.clip(jax.random.normal(fourth, shape, jnp.float32), -5.0, 5.0) * 0.5 * jnp.power(3.0, level)
    return jnp.stack([keys, values], axis=1).astype(jnp.bfloat16)


def draw_sequence_history_count(key, part):
    key = jax.random.fold_in(key, 37)
    first, second = jax.random.split(key)
    longest = PAGES_REQ * PAGE_TOKENS
    lengths = jax.random.randint(first, (REQS,), 1, longest + 1)
    full = jax.random.randint(second, (), 0, REQS)
    return jnp.where(jnp.arange(REQS) == full, longest, lengths).astype(jnp.int32)


def touch_ends(array, stream_key, smallest, top_value):
    shape = array.shape
    spot = [jax.random.randint(jax.random.fold_in(stream_key, axis), (), 0, shape[axis]) for axis in range(len(shape))]
    array = array.at[tuple(spot)].set(smallest)
    longest = shape.index(max(shape))
    spot[longest] = (spot[longest] + 1) % shape[longest]
    return array.at[tuple(spot)].set(top_value)


def block_levels(stream_key, dims, shards, low, top_value):
    level, own = 1.0, jax.random.fold_in(stream_key, 6)
    for dim, blocks in shards:
        steps = jnp.exp(jax.random.uniform(jax.random.fold_in(own, dim), (blocks,), jnp.float32, low / len(shards), top_value / len(shards)))
        level = level * jnp.repeat(steps, dims[dim] // blocks).reshape([-1 if axis == dim else 1 for axis in range(len(dims))])
    return level


def routed_block(own_key, own, number, rows, amount, top, limit, lean):
    order = jax.random.permutation(own_key, amount)
    crowded, ordinary = portions_of(amount, rows * top, limit, lean, True), portions_of(amount, rows * top, limit, lean, False)
    places = jnp.arange(amount)

    def named(sizes, rotation):
        used = int((sizes > 0).sum())
        fixed = max(1, used // 4)
        moved = fixed + (places - fixed + rotation * (used - fixed)) % max(1, amount - fixed)
        return jnp.zeros((amount,), jnp.int32).at[order[jnp.where(places < fixed, places, moved)]].set(jnp.asarray(sizes, jnp.int32))

    sizes = jnp.where(number % 4 == 0, named(crowded, number // 4), named(ordinary, number - number // 4 - 1))
    mixed = jax.random.permutation(jax.random.fold_in(own, 3), amount)
    giver, sink = mixed[0:amount // 2 * 2:2], mixed[1:amount // 2 * 2:2]
    margin = jnp.minimum(sizes[giver] - 1, limit - sizes[sink]) // 2
    margin = jnp.where((giver == order[0]) | (sink == order[0]) | (sizes[sink] == 0), 0, jnp.maximum(margin, 0))
    moved = jax.random.randint(jax.random.fold_in(own, 4), (amount // 2,), 0, 1 << 20) % (margin + 1)
    sizes = sizes.at[giver].add(-moved).at[sink].add(moved)
    labels = jnp.searchsorted(jnp.cumsum(sizes), jnp.arange(rows * top), side="right").astype(jnp.int32)
    listing = labels.reshape(top, rows).T
    listing = listing[jax.random.permutation(jax.random.fold_in(own, 1), rows)]
    rotation = jax.random.randint(jax.random.fold_in(own, 2), (rows, 1), 0, top)
    return jnp.take_along_axis(listing, (jnp.arange(top)[None, :] + rotation) % top, axis=1)


def portions_of(count, total, reach, lean, full):
    portions = [(1 << 20) // math.isqrt(rank ** lean) + 1 for rank in range(1, count + 1)]
    largest = reach if full else min(reach, max(-(-total // count), total * portions[0] // sum(portions)))
    least = 1 if total - largest >= count - 1 else 0
    counts, spare = [largest] + [least] * (count - 1), total - largest - least * (count - 1)
    while spare > 0:
        candidates = [i for i in range(1, count) if counts[i] < largest] or [i for i in range(1, count) if counts[i] < reach]
        pool, remaining = sum([portions[i] for i in candidates]), spare
        for i in candidates:
            addition = min(reach - counts[i], max(1, remaining * portions[i] // pool), spare)
            counts[i] = counts[i] + addition
            spare = spare - addition
    return np.array(counts)


def scatter_about(own_key, dims, scale, limit, cuts=(), kind=jnp.bfloat16):
    gain = block_levels(own_key, dims, cuts, -0.22, 0.18) if cuts else 1.0
    values = jax.random.normal(own_key, dims, jnp.float32) * scale * gain
    return jnp.minimum(jnp.maximum(values, -limit), limit).astype(kind)


def setup_inputs(seed: int = 0) -> dict:
    key_list = jax.random.split(jax.random.key(seed), 12)
    lookup_vectors = draw_lookup_vectors(jax.random.fold_in(key_list[11], 71), 0)
    fresh_token_memory = scatter_about(key_list[1], (DECODE_STEP_COUNT, REQS, 2, KVH, HD), 1.0, 5.0, ((1, 16), (3, 2)))
    unfinished_block_memory = scatter_about(key_list[2], (REQS, 2, PAGE_TOKENS, KVH, HD), 1.0, 5.0, ((0, 16), (3, 2)))
    cache_block_store = draw_cache_block_store(jax.random.fold_in(key_list[11], 71), 0)
    sequence_block_index = touch_ends(jax.random.randint(key_list[4], (REQS, PAGES_REQ), 0, POOL_PAGE_COUNT + ARRIVE), jax.random.fold_in(key_list[4], 1), 0, (POOL_PAGE_COUNT + ARRIVE) - 1).astype(jnp.int32)
    sequence_history_count = draw_sequence_history_count(jax.random.fold_in(key_list[11], 71), 0)
    unfinished_block_fill = touch_ends(jax.random.randint(key_list[6], (REQS,), 0, PAGE_TOKENS - DECODE_STEP_COUNT + 1), jax.random.fold_in(key_list[6], 1), 0, PAGE_TOKENS - DECODE_STEP_COUNT).astype(jnp.int32)
    migration_sender_block = touch_ends(jax.random.randint(key_list[7], (MIGS,), 0, POOL_PAGE_COUNT + REQ_DEV), jax.random.fold_in(key_list[7], 1), 0, (POOL_PAGE_COUNT + REQ_DEV) - 1).astype(jnp.int32)
    migration_receiver_server_keys = jax.random.split(jax.random.fold_in(key_list[8], 1), MIGS // MIG_DEV)
    migration_receiver_server_turns = jax.random.permutation(jax.random.fold_in(key_list[8], 3), MIGS // MIG_DEV)
    migration_receiver_server = jax.vmap(lambda own, number: routed_block(jax.random.fold_in(key_list[8], 2), own, number, MIG_DEV, N_REP, 1, CAP, 2))(migration_receiver_server_keys, migration_receiver_server_turns).reshape((MIGS, 1))
    switch_moment = touch_ends(jax.random.randint(key_list[9], (REQS,), 0, DECODE_STEP_COUNT + 1), jax.random.fold_in(key_list[9], 1), 0, DECODE_STEP_COUNT).astype(jnp.int32)
    output_scaling_weights = jnp.clip(1.0 + 0.1 * jax.random.normal(key_list[10], (H * HD,), jnp.float32), 0.5, 1.5)
    return dict(lookup_vectors=lookup_vectors, fresh_token_memory=fresh_token_memory, unfinished_block_memory=unfinished_block_memory, cache_block_store=cache_block_store, sequence_block_index=sequence_block_index, sequence_history_count=sequence_history_count, unfinished_block_fill=unfinished_block_fill, migration_sender_block=migration_sender_block, migration_receiver_server=migration_receiver_server, switch_moment=switch_moment, output_scaling_weights=output_scaling_weights)


def filled_tail(unfinished_block_memory, fresh_token_memory, unfinished_block_fill):
    decode_steps = fresh_token_memory.shape[0]
    page_entry = unfinished_block_memory.shape[2]
    offsets = jnp.arange(page_entry, dtype=jnp.int32)
    hits = offsets[None, None, :] == unfinished_block_fill[None, :, None] + jnp.arange(decode_steps, dtype=jnp.int32)[:, None, None]
    placed = jnp.einsum('srp,srckd->rcpkd', hits.astype(jnp.float32), fresh_token_memory.astype(jnp.float32))
    covered = jnp.any(hits, axis=0)
    merged = jnp.where(covered[:, None, :, None, None], placed, unfinished_block_memory.astype(jnp.float32))
    return merged.astype(jnp.bfloat16)

def slot_ranks(target):
    order = jnp.arange(target.shape[0], dtype=jnp.int32)
    same = (target[:, None] == target[None, :]) & (order[None, :] < order[:, None])
    return lax.optimization_barrier(jnp.sum(same.astype(jnp.int32), axis=1, dtype=jnp.int32))

def token_validity(page_table_row, context_length, arrival_length, tail_length, boundary_marker, pool_page_tiles, page_entry, decode_steps):
    entry = jnp.repeat(page_table_row, page_entry)
    position = jnp.arange(entry.shape[0], dtype=jnp.int32)
    offset = position % page_entry
    incoming = entry >= pool_page_tiles
    known = arrival_length[jnp.clip(entry - pool_page_tiles, 0, arrival_length.shape[0] - 1)]
    step = jnp.arange(decode_steps, dtype=jnp.int32)[:, None]
    page_ok = (position < context_length)[None, :] & (jnp.logical_not(incoming)[None, :] | (step >= boundary_marker) & (offset < known)[None, :])
    tail_ok = jnp.arange(page_entry, dtype=jnp.int32)[None, :] < tail_length + step + 1
    return jnp.concatenate([page_ok, tail_ok], axis=1)

def attend(query_vector, pages, tail_block, valid_mask):
    decode_steps, heads, hdim = query_vector.shape
    kv_heads = pages.shape[3]
    keys = jnp.concatenate([pages[:, 0].reshape(-1, kv_heads, hdim), tail_block[0]], 0)
    values = jnp.concatenate([pages[:, 1].reshape(-1, kv_heads, hdim), tail_block[1]], 0)
    grouped = query_vector.reshape(decode_steps, kv_heads, heads // kv_heads, hdim)
    scores = jnp.einsum('skgd,lkd->skgl', grouped.astype(jnp.float32), keys.astype(jnp.float32)) / math.sqrt(hdim)
    scores = jnp.where(valid_mask[:, None, None, :], scores, -jnp.inf)
    top = lax.optimization_barrier(jnp.max(scores, axis=-1, keepdims=True))
    probs = jnp.exp(scores - top)
    total = lax.optimization_barrier(jnp.sum(probs, axis=-1, keepdims=True))
    weights = probs.astype(jnp.bfloat16)
    mixed = jnp.einsum('skgl,lkd->skgd', weights.astype(jnp.float32), values.astype(jnp.float32)) / total
    return mixed.reshape(decode_steps, heads, hdim).astype(jnp.bfloat16)

def reference(lookup_vectors, fresh_token_memory, unfinished_block_memory, cache_block_store, sequence_block_index, sequence_history_count, unfinished_block_fill, migration_sender_block, migration_receiver_server, switch_moment, output_scaling_weights):
    tails = filled_tail(unfinished_block_memory, fresh_token_memory, unfinished_block_fill)
    source = migration_sender_block.reshape(N_REP, MIG_DEV)
    target = migration_receiver_server.reshape(N_REP, MIG_DEV)
    ranks = jax.vmap(slot_ranks)(target)
    anchor = jnp.arange(N_REP, dtype=jnp.int32)[:, None]
    landing = (target * ARRIVE + anchor * CAP + ranks).reshape(-1)
    from_tail = (source >= POOL_PAGE_COUNT).reshape(-1)
    pool_pick = (anchor * POOL_PAGE_COUNT + jnp.clip(source, 0, POOL_PAGE_COUNT - 1)).reshape(-1)
    tail_pick = (anchor * REQ_DEV + jnp.clip(source - POOL_PAGE_COUNT, 0, REQ_DEV - 1)).reshape(-1)
    lengths = jnp.where(from_tail, unfinished_block_fill[tail_pick] + switch_moment[tail_pick], PAGE_TOKENS).astype(jnp.int32)
    slots = N_REP * ARRIVE
    slot_pool = jnp.zeros((slots,), jnp.int32).at[landing].set(pool_pick.astype(jnp.int32))
    slot_tail = jnp.zeros((slots,), jnp.int32).at[landing].set(tail_pick.astype(jnp.int32))
    slot_flag = jnp.zeros((slots,), jnp.int32).at[landing].set(from_tail.astype(jnp.int32))
    slot_len = jnp.zeros((slots,), jnp.int32).at[landing].set(lengths)

    def one_replica(replica):
        start = (replica * ARRIVE).astype(jnp.int32)
        pick_pool = lax.dynamic_slice_in_dim(slot_pool, start, ARRIVE)
        pick_tail = lax.dynamic_slice_in_dim(slot_tail, start, ARRIVE)
        pick_flag = lax.dynamic_slice_in_dim(slot_flag, start, ARRIVE)
        selected_length = lax.dynamic_slice_in_dim(slot_len, start, ARRIVE)
        arrivals = jnp.where((pick_flag > 0)[:, None, None, None, None], tails[pick_tail], cache_block_store[pick_pool])
        arrivals = jnp.where((selected_length > 0)[:, None, None, None, None], arrivals, jnp.zeros_like(arrivals))
        own = lax.dynamic_slice_in_dim(cache_block_store, (replica * POOL_PAGE_COUNT).astype(jnp.int32), POOL_PAGE_COUNT)
        extended = jnp.concatenate([own, arrivals], 0)
        first = (replica * REQ_DEV).astype(jnp.int32)
        rows_query = lax.dynamic_slice_in_dim(lookup_vectors, first, REQ_DEV, 1)
        rows_table = lax.dynamic_slice_in_dim(sequence_block_index, first, REQ_DEV)
        rows_tail = lax.dynamic_slice_in_dim(tails, first, REQ_DEV)
        rows_ctx = lax.dynamic_slice_in_dim(sequence_history_count, first, REQ_DEV)
        rows_tlen = lax.dynamic_slice_in_dim(unfinished_block_fill, first, REQ_DEV)
        rows_switch = lax.dynamic_slice_in_dim(switch_moment, first, REQ_DEV)

        def one_request(request_element):
            query_vector, page_table_row, tail_block, context_length, tail_length, handover_step = request_element
            valid_mask = token_validity(page_table_row, context_length, selected_length, tail_length, handover_step, POOL_PAGE_COUNT, PAGE_TOKENS, DECODE_STEP_COUNT)
            return attend(query_vector, extended[page_table_row], tail_block, valid_mask)
        return lax.map(one_request, (jnp.transpose(rows_query, (1, 0, 2, 3)), rows_table, rows_tail, rows_ctx, rows_tlen, rows_switch))
    mixed = lax.map(one_replica, jnp.arange(N_REP, dtype=jnp.int32))
    attn = jnp.transpose(mixed.reshape(REQS, DECODE_STEP_COUNT, H * HD), (1, 0, 2))
    wide = attn.astype(jnp.float32)
    mean = lax.optimization_barrier(jnp.sum(wide * wide, axis=-1, keepdims=True)) / (H * HD)
    return (wide * lax.rsqrt(mean + 1e-05) * output_scaling_weights).astype(jnp.bfloat16)
```

```python
import functools
import math

import jax
import jax.numpy as jnp
from jax import lax
from jax.experimental import pallas as pl
from jax.experimental.pallas import tpu as pltpu
from jax.sharding import PartitionSpec as P

NEG = -1e30
LOG2E = 1.4426950408889634
VMEM_LIMIT = 50 * 1024 * 1024


def pack_kernel(cap, sender, target, lengths, tiles, out, held):
    replicas = out.shape[0]
    pool = tiles.shape[0] - lengths.shape[0]
    parts, kv, page, hdim = tiles.shape[1:]
    for d in range(replicas):
        held[d] = 0
    lane = lax.broadcasted_iota(jnp.int32, (page, hdim), 1)
    out[...] = jnp.zeros_like(out)

    def place(e, carry):
        d = target[e, 0]
        rank = held[d]
        held[d] = rank + 1
        source = sender[e]
        for c in range(parts):
            for k in range(kv):
                out[d, (c * kv + k) * cap + rank] = tiles[source, c, k]
        from_tail = source >= pool
        length = jnp.where(from_tail, lengths[jnp.maximum(source - pool, 0)], page)
        inside = (lane >= rank * page) & (lane < rank * page + length)
        mask = out[d, parts * kv * cap]
        out[d, parts * kv * cap] = jnp.where(inside, 1.0, mask.astype(jnp.float32)).astype(mask.dtype)
        return carry

    lax.fori_loop(0, sender.shape[0], place, 0)


def pack(tiles, sender, target, lengths, replicas, cap):
    _, parts, kv, page, hdim = tiles.shape
    smem = pl.BlockSpec(memory_space=pltpu.SMEM)
    vmem = pl.BlockSpec(memory_space=pltpu.VMEM)
    return pl.pallas_call(
        functools.partial(pack_kernel, cap),
        out_shape=jax.ShapeDtypeStruct((replicas, parts * kv * cap + 1, page, hdim), tiles.dtype),
        in_specs=[smem, smem, smem, vmem],
        out_specs=vmem,
        scratch_shapes=[pltpu.SMEM((replicas,), jnp.int32)],
        compiler_params=pltpu.CompilerParams(vmem_limit_bytes=VMEM_LIMIT),
        name="pack",
    )(sender, target, lengths, tiles)


def counts_of(table, history, first, pages, page):
    requests, entries = table.shape
    offset = lax.broadcasted_iota(jnp.int32, (page, entries), 0)
    position = lax.broadcasted_iota(jnp.int32, (page, entries), 1) * page + offset
    named = lax.broadcasted_iota(jnp.int32, (pages, entries), 0) + first
    per_page = []
    for g in range(requests):
        inside = jnp.where(position < history[g], 1.0, 0.0).astype(jnp.bfloat16)
        hit = jnp.where(table[g : g + 1, :] == named, 1.0, 0.0).astype(jnp.bfloat16)
        per_page.append(
            lax.dot_general(inside, hit, (((1,), (1,)), ((), ())), preferred_element_type=jnp.float32)
        )
    tokens = pages * page
    spread = (
        lax.broadcasted_iota(jnp.int32, (pages, tokens), 1) // page
        == lax.broadcasted_iota(jnp.int32, (pages, tokens), 0)
    )
    wide = jnp.dot(
        jnp.concatenate(per_page, 0).astype(jnp.bfloat16),
        jnp.where(spread, 1.0, 0.0).astype(jnp.bfloat16),
        preferred_element_type=jnp.float32,
    )
    own = (
        lax.broadcasted_iota(jnp.int32, (page, tokens), 1) % page
        == lax.broadcasted_iota(jnp.int32, (page, tokens), 0)
    )
    return [
        jnp.sum(jnp.where(own, wide[g * page : (g + 1) * page], 0.0), axis=0, keepdims=True)
        for g in range(requests)
    ]


def bias_of(count):
    return jnp.where(count > 0.0, jnp.log2(jnp.maximum(count, 1.0)), NEG)


def head_scores(query, keys, bias):
    rows, hdim = query.shape
    scores = lax.dot_general(query, keys, (((1,), (1,)), ((), ())), preferred_element_type=jnp.float32)
    groups = bias.shape[0]
    scores = scores.reshape(groups, rows // groups, -1) * (LOG2E / math.sqrt(hdim)) + bias[:, None, :]
    return scores.reshape(rows, -1)


def pool_kernel(history, fill, table, query, tiles, mixed, top, total, bias):
    steps, requests, heads, hdim = query.shape
    all_pages, _, kv, page, _ = tiles.shape
    pool = all_pages - requests
    counts = counts_of(table, history, 0, pool, page)
    tail = lax.broadcasted_iota(jnp.int32, (1, requests * page), 1)
    for t in range(steps):
        for g in range(requests):
            row = t * requests + g
            bias[row : row + 1, : pool * page] = bias_of(counts[g])
            seen = (tail // page == g) & (tail % page < fill[g] + t + 1)
            bias[row : row + 1, pool * page :] = jnp.where(seen, 0.0, NEG)
    group = heads // kv
    rows = steps * requests * group

    def one_head(k, carry):
        q = query[:, :, pl.ds(k * group, group), :].reshape(rows, hdim)
        keys = tiles[:, 0, k].reshape(all_pages * page, hdim)
        values = tiles[:, 1, k].reshape(all_pages * page, hdim)
        scores = head_scores(q, keys, bias[...])
        best = jnp.max(scores, axis=-1, keepdims=True)
        probs = jnp.exp2(scores - best)
        total[k] = jnp.sum(probs, axis=-1, keepdims=True)
        top[k] = best
        mixed[k] = jnp.dot(probs.astype(jnp.bfloat16), values, preferred_element_type=jnp.float32)
        return carry

    lax.fori_loop(0, kv, one_head, 0)


def attend_pool(query, tiles, table, history, fill):
    steps, requests, heads, hdim = query.shape
    all_pages, _, kv, page, _ = tiles.shape
    rows = steps * requests * heads // kv
    smem = pl.BlockSpec(memory_space=pltpu.SMEM)
    vmem = pl.BlockSpec(memory_space=pltpu.VMEM)
    one = jax.ShapeDtypeStruct((kv, rows, 1), jnp.float32)
    flops = 4 * kv * rows * all_pages * page * hdim
    return pl.pallas_call(
        pool_kernel,
        out_shape=(jax.ShapeDtypeStruct((kv, rows, hdim), jnp.float32), one, one),
        in_specs=[smem, smem, vmem, vmem, vmem],
        out_specs=(vmem, vmem, vmem),
        scratch_shapes=[pltpu.VMEM((steps * requests, all_pages * page), jnp.float32)],
        compiler_params=pltpu.CompilerParams(vmem_limit_bytes=VMEM_LIMIT),
        cost_estimate=pl.CostEstimate(flops=8 * flops, bytes_accessed=8 << 20, transcendentals=0),
        name="attend_pool",
    )(history, fill, table, query, tiles)


def arrival_kernel(cap, pool, history, switch, table, query, arrived, mixed0, top0, total0, attn, square, bias):
    steps, requests, heads, hdim = query.shape
    replicas = arrived.shape[0]
    kv, page = mixed0.shape[0], arrived.shape[2]
    tokens = replicas * cap * page
    counts = counts_of(table, history, pool, replicas * cap, page)
    here = arrived[:, 2 * kv * cap, 0, :]
    width = cap * page
    repeat = (
        lax.broadcasted_iota(jnp.int32, (hdim, tokens), 1) % width
        == lax.broadcasted_iota(jnp.int32, (hdim, tokens), 0)
    )
    spread = jnp.dot(here, jnp.where(repeat, 1.0, 0.0).astype(jnp.bfloat16), preferred_element_type=jnp.float32)
    mine = (
        lax.broadcasted_iota(jnp.int32, (replicas, tokens), 1) // width
        == lax.broadcasted_iota(jnp.int32, (replicas, tokens), 0)
    )
    filled = jnp.sum(jnp.where(mine, spread, 0.0), axis=0, keepdims=True)
    for g in range(requests):
        usable = bias_of(counts[g] * filled)
        for t in range(steps):
            row = t * requests + g
            bias[row : row + 1, :] = jnp.where(t >= switch[g], usable, NEG)
    group = heads // kv
    rows = steps * requests * group
    square[...] = jnp.zeros_like(square)

    def one_head(k, carry):
        q = query[:, :, pl.ds(k * group, group), :].reshape(rows, hdim)
        keys = arrived[:, pl.ds(k * cap, cap)].reshape(tokens, hdim)
        values = arrived[:, pl.ds((kv + k) * cap, cap)].reshape(tokens, hdim)
        scores = head_scores(q, keys, bias[...])
        before = top0[k]
        best = jnp.maximum(jnp.max(scores, axis=-1, keepdims=True), before)
        probs = jnp.exp2(scores - best)
        kept = jnp.exp2(before - best)
        total = jnp.sum(probs, axis=-1, keepdims=True) + total0[k] * kept
        out = jnp.dot(probs.astype(jnp.bfloat16), values, preferred_element_type=jnp.float32)
        out = ((out + mixed0[k] * kept) / total).astype(jnp.bfloat16)
        attn[:, :, pl.ds(k * group, group), :] = out.reshape(steps, requests, group, hdim)
        wide = out.astype(jnp.float32)
        square[...] += jnp.sum((wide * wide).reshape(steps * requests, group, hdim), axis=1)
        return carry

    lax.fori_loop(0, kv, one_head, 0)


def attend_arrivals(query, arrived, table, history, switch, mixed, top, total, cap, pool):
    steps, requests, heads, hdim = query.shape
    replicas, _, page, _ = arrived.shape
    smem = pl.BlockSpec(memory_space=pltpu.SMEM)
    vmem = pl.BlockSpec(memory_space=pltpu.VMEM)
    return pl.pallas_call(
        functools.partial(arrival_kernel, cap, pool),
        out_shape=(
            jax.ShapeDtypeStruct(query.shape, jnp.bfloat16),
            jax.ShapeDtypeStruct((steps * requests, hdim), jnp.float32),
        ),
        in_specs=[smem, smem] + [vmem] * 6,
        out_specs=(vmem, vmem),
        scratch_shapes=[pltpu.VMEM((steps * requests, replicas * cap * page), jnp.float32)],
        compiler_params=pltpu.CompilerParams(vmem_limit_bytes=VMEM_LIMIT),
        name="attend_arrivals",
    )(history, switch, table, query, arrived, mixed, top, total)


def filled_tail(unfinished, fresh, fill):
    offset = jnp.arange(unfinished.shape[2], dtype=jnp.int32)[None, None, :, None, None]
    out = unfinished
    for s in range(fresh.shape[0]):
        out = jnp.where(offset == fill[:, None, None, None, None] + s, fresh[s][:, :, None], out)
    return out


def body(query, fresh, unfinished, store, table, history, fill, sender, target, switch, gain):
    replicas = lax.axis_size("rep")
    steps, requests, heads, hdim = query.shape
    pool = store.shape[0]
    cap = max(2, 2 * sender.shape[0] // replicas)
    tiles = jnp.concatenate([store, filled_tail(unfinished, fresh, fill)], 0)
    tiles = jnp.transpose(tiles, (0, 1, 3, 2, 4))
    outgoing = pack(tiles, sender, target, fill + switch, replicas, cap)
    arrived = lax.all_to_all(outgoing, "rep", split_axis=0, concat_axis=0, tiled=True)
    mixed, top, total = attend_pool(query, tiles, table, history, fill)
    attn, square = attend_arrivals(
        query, arrived, table, history, switch, mixed, top, total, cap, pool
    )
    square = lax.psum(jnp.sum(square, axis=-1).reshape(steps, requests, 1), "tp")
    width = heads * hdim * lax.axis_size("tp")
    wide = attn.reshape(steps, requests, heads * hdim).astype(jnp.float32)
    return (wide * lax.rsqrt(square / width + 1e-05) * gain).astype(jnp.bfloat16)


def solution(mesh):
    placed = (
        P(None, "rep", "tp", None),
        P(None, "rep", None, "tp", None),
        P("rep", None, None, "tp", None),
        P("rep", None, None, "tp", None),
        P("rep", None),
        P("rep"),
        P("rep"),
        P("rep"),
        P("rep", None),
        P("rep"),
        P("tp"),
    )
    return jax.shard_map(
        body, mesh=mesh, in_specs=placed, out_specs=P(None, "rep", "tp"), check_vma=False
    )
```

```python
import functools
import math

import jax
import jax.numpy as jnp
from jax import lax
from jax.experimental import pallas as pl
from jax.experimental.pallas import tpu as pltpu
from jax.sharding import PartitionSpec as P

NEG = -1e30
LOG2E = 1.4426950408889634
VMEM_LIMIT = 50 * 1024 * 1024


def counts_of(table, history, first, pages, page):
    requests, entries = table.shape
    offset = lax.broadcasted_iota(jnp.int32, (page, entries), 0)
    position = lax.broadcasted_iota(jnp.int32, (page, entries), 1) * page + offset
    named = lax.broadcasted_iota(jnp.int32, (pages, entries), 0) + first
    per_page = []
    for g in range(requests):
        inside = jnp.where(position < history[g], 1.0, 0.0).astype(jnp.bfloat16)
        hit = jnp.where(table[g : g + 1, :] == named, 1.0, 0.0).astype(jnp.bfloat16)
        per_page.append(
            lax.dot_general(inside, hit, (((1,), (1,)), ((), ())), preferred_element_type=jnp.float32)
        )
    tokens = pages * page
    spread = (
        lax.broadcasted_iota(jnp.int32, (pages, tokens), 1) // page
        == lax.broadcasted_iota(jnp.int32, (pages, tokens), 0)
    )
    wide = jnp.dot(
        jnp.concatenate(per_page, 0).astype(jnp.bfloat16),
        jnp.where(spread, 1.0, 0.0).astype(jnp.bfloat16),
        preferred_element_type=jnp.float32,
    )
    own = (
        lax.broadcasted_iota(jnp.int32, (page, tokens), 1) % page
        == lax.broadcasted_iota(jnp.int32, (page, tokens), 0)
    )
    return [
        jnp.sum(jnp.where(own, wide[g * page : (g + 1) * page], 0.0), axis=0, keepdims=True)
        for g in range(requests)
    ]


def bias_of(count):
    return jnp.where(count > 0.0, jnp.log2(jnp.maximum(count, 1.0)), NEG)


def head_scores(query, keys, bias):
    rows, hdim = query.shape
    scores = lax.dot_general(query, keys, (((1,), (1,)), ((), ())), preferred_element_type=jnp.float32)
    groups = bias.shape[0]
    scores = scores.reshape(groups, rows // groups, -1) * (LOG2E / math.sqrt(hdim)) + bias[:, None, :]
    return scores.reshape(rows, -1)


def pack_kernel(cap, plane, sender, target, history, fill, switch, tiles, table, out, count, bias, held):
    replicas = out.shape[0]
    requests = fill.shape[0]
    pool = tiles.shape[0] - requests
    parts, kv, page, hdim = tiles.shape[1:]
    steps = bias.shape[0] // requests
    for d in range(replicas):
        held[d] = 0
    lane = lax.broadcasted_iota(jnp.int32, (page, hdim), 1)
    out[...] = jnp.zeros_like(out)

    def place(e, carry):
        d = target[e, 0]
        rank = held[d]
        held[d] = rank + 1
        source = sender[e]
        for c in range(parts):
            for k in range(kv):
                out[d, (c * kv + k) * cap + rank] = tiles[source, c, k]
        owner = jnp.maximum(source - pool, 0)
        length = jnp.where(source >= pool, fill[owner] + switch[owner], page)
        inside = (lane >= rank * page) & (lane < rank * page + length)
        mask = out[d, parts * kv * cap]
        out[d, parts * kv * cap] = jnp.where(inside, 1.0, mask.astype(jnp.float32)).astype(mask.dtype)
        return carry

    lax.fori_loop(0, sender.shape[0], place, 0)
    own = counts_of(table, history, 0, pool, page)
    tail = lax.broadcasted_iota(jnp.int32, (1, requests * page), 1)
    arrivals = counts_of(table, history, pool, replicas * cap, page)
    width = plane * cap * page
    for t in range(steps):
        for g in range(requests):
            row = t * requests + g
            bias[row : row + 1, : pool * page] = bias_of(own[g])
            seen = (tail // page == g) & (tail % page < fill[g] + t + 1)
            bias[row : row + 1, pool * page :] = jnp.where(seen, 0.0, NEG)
    for line in range(replicas // plane):
        rows = []
        for t in range(steps):
            for g in range(requests):
                part = arrivals[g][:, line * width : (line + 1) * width]
                rows.append(jnp.where(t >= switch[g], part, 0.0))
        count[line] = jnp.concatenate(rows, 0).astype(count.dtype)


def pack(tiles, sender, target, table, history, fill, switch, steps, replicas, cap, plane):
    pages, parts, kv, page, hdim = tiles.shape
    requests = fill.shape[0]
    smem = pl.BlockSpec(memory_space=pltpu.SMEM)
    vmem = pl.BlockSpec(memory_space=pltpu.VMEM)
    return pl.pallas_call(
        functools.partial(pack_kernel, cap, plane),
        out_shape=(
            jax.ShapeDtypeStruct((replicas, parts * kv * cap + 1, page, hdim), tiles.dtype),
            jax.ShapeDtypeStruct((replicas // plane, steps * requests, plane * cap * page), jnp.bfloat16),
            jax.ShapeDtypeStruct((steps * requests, pages * page), jnp.float32),
        ),
        in_specs=[smem] * 5 + [vmem] * 2,
        out_specs=(vmem, vmem, vmem),
        scratch_shapes=[pltpu.SMEM((replicas,), jnp.int32)],
        compiler_params=pltpu.CompilerParams(vmem_limit_bytes=VMEM_LIMIT),
        name="pack",
    )(sender, target, history, fill, switch, tiles, table)


def partial(query, keys, values, bias):
    scores = head_scores(query, keys, bias)
    best = jnp.max(scores, axis=-1, keepdims=True)
    probs = jnp.exp2(scores - best)
    total = jnp.sum(probs, axis=-1, keepdims=True)
    return jnp.dot(probs.astype(jnp.bfloat16), values, preferred_element_type=jnp.float32), best, total


def diagonal(size):
    return lax.broadcasted_iota(jnp.int32, (size, size), 0) == lax.broadcasted_iota(jnp.int32, (size, size), 1)


def attend_kernel(
    cap, plane, lines, total_width,
    query, count, bias, gain, tiles, outgoing,
    out,
    arrived, asked, asked_count, answer, answer_log, given, given_log, mixed, top, total, attn, square,
    own_sem, tile_send, tile_recv, ask_send, ask_recv, count_send, count_recv,
    answer_send, answer_recv, log_send, log_recv, square_sem,
):
    steps, requests, heads, hdim = query.shape
    all_pages, _, kv, page, _ = tiles.shape
    group = heads // kv
    groups = steps * requests
    rows = groups * group
    tokens = plane * cap * page
    me = lax.axis_index("rep")
    core = lax.axis_index("tp")
    line, place = lax.div(me, plane), lax.rem(me, plane)

    def peer(a_line, a_place):
        return {"rep": a_line * plane + a_place}

    def send(source, target, send_sem, recv_sem, device):
        return pltpu.make_async_remote_copy(
            src_ref=source, dst_ref=target, send_sem=send_sem, recv_sem=recv_sem,
            device_id=device, device_id_type=pl.DeviceIdType.MESH,
        )

    def line_at(step):
        return lax.rem(line + step, lines)

    def line_back(step):
        return lax.rem(line + lines - step, lines)

    def place_at(step):
        return lax.rem(place + step, plane)

    barrier = pltpu.get_barrier_semaphore()
    for j in range(1, lines):
        pl.semaphore_signal(barrier, inc=1, device_id=peer(line_at(j), place), device_id_type=pl.DeviceIdType.MESH)
    for i in range(1, plane):
        pl.semaphore_signal(barrier, inc=1, device_id=peer(line, place_at(i)), device_id_type=pl.DeviceIdType.MESH)
    pl.semaphore_signal(barrier, inc=1, device_id={"tp": 1 - core}, device_id_type=pl.DeviceIdType.MESH)
    pl.semaphore_wait(barrier, lines + plane - 1)

    def ask(j):
        to = line_at(j)
        return (
            send(query, asked.at[line], ask_send.at[to], ask_recv.at[line], peer(to, place)),
            send(count.at[to], asked_count.at[line], count_send.at[to], count_recv.at[line], peer(to, place)),
        )

    def ship(j, i):
        to = line_at(j)
        mate = place_at(i)
        return send(
            outgoing.at[to * plane + mate], arrived.at[to, place],
            tile_send.at[to, mate], tile_recv.at[to, place], peer(line, mate),
        )

    def keep(j):
        to = line_at(j)
        return pltpu.make_async_copy(outgoing.at[to * plane + place], arrived.at[to, place], own_sem.at[to])

    def reply(j):
        to = line_at(j)
        return (
            send(answer.at[to], given.at[line], answer_send.at[to], answer_recv.at[line], peer(to, place)),
            send(answer_log.at[to], given_log.at[line], log_send.at[to], log_recv.at[line], peer(to, place)),
        )

    for j in range(1, lines + 1):
        for i in range(1, plane):
            ship(j, i).start()
        keep(j).start()
        if j < lines:
            for copy in ask(lines - j):
                copy.start()

    def pool_head(k, carry):
        q = query[:, :, pl.ds(k * group, group), :].reshape(rows, hdim)
        keys = tiles[:, 0, k].reshape(all_pages * page, hdim)
        values = tiles[:, 1, k].reshape(all_pages * page, hdim)
        mixed[k], top[k], total[k] = partial(q, keys, values, bias[...])
        return carry

    lax.fori_loop(0, kv, pool_head, 0)

    width = cap * page
    repeat = (
        lax.broadcasted_iota(jnp.int32, (hdim, tokens), 1) % width
        == lax.broadcasted_iota(jnp.int32, (hdim, tokens), 0)
    )
    repeat = jnp.where(repeat, 1.0, 0.0).astype(jnp.bfloat16)
    mine = (
        lax.broadcasted_iota(jnp.int32, (plane, tokens), 1) // width
        == lax.broadcasted_iota(jnp.int32, (plane, tokens), 0)
    )
    eye = diagonal(rows)

    def filled(to):
        here = arrived[to, :, 2 * kv * cap, 0, :]
        spread = jnp.dot(here, repeat, preferred_element_type=jnp.float32)
        return jnp.sum(jnp.where(mine, spread, 0.0), axis=0, keepdims=True)

    def arrivals(to, k):
        keys = arrived[to, :, pl.ds(k * cap, cap)].reshape(tokens, hdim)
        values = arrived[to, :, pl.ds((kv + k) * cap, cap)].reshape(tokens, hdim)
        return keys, values

    for j in range(1, lines):
        to = line_at(j)
        for i in range(1, plane):
            source = place_at(i)
            send(
                outgoing.at[0], arrived.at[to, source], tile_send.at[to, source], tile_recv.at[to, source],
                peer(line, source),
            ).wait_recv()
        keep(j).wait()
        send(query, asked.at[to], ask_send.at[to], ask_recv.at[to], peer(to, place)).wait_recv()
        send(
            count.at[to], asked_count.at[to], count_send.at[to], count_recv.at[to], peer(to, place)
        ).wait_recv()
        set_bias = bias_of(asked_count[to].astype(jnp.float32) * filled(to))

        def set_head(k, carry):
            q = asked[to, :, :, pl.ds(k * group, group), :].reshape(rows, hdim)
            keys, values = arrivals(to, k)
            part, best, amount = partial(q, keys, values, set_bias)
            answer[to, k] = (part / amount).astype(jnp.bfloat16)
            log = best + jnp.log2(amount)
            answer_log[to, k] = jnp.sum(jnp.where(eye, log, 0.0), axis=0, keepdims=True)
            return carry

        lax.fori_loop(0, kv, set_head, 0)
        for copy in reply(j):
            copy.start()

    for i in range(1, plane):
        source = place_at(i)
        send(
            outgoing.at[0], arrived.at[line, source], tile_send.at[line, source], tile_recv.at[line, source],
            peer(line, source),
        ).wait_recv()
    keep(lines).wait()
    last_bias = bias_of(count[line].astype(jnp.float32) * filled(line))

    def last_head(k, carry):
        q = query[:, :, pl.ds(k * group, group), :].reshape(rows, hdim)
        keys, values = arrivals(line, k)
        part, best, amount = partial(q, keys, values, last_bias)
        high = jnp.maximum(best, top[k])
        fresh, old = jnp.exp2(best - high), jnp.exp2(top[k] - high)
        mixed[k] = part * fresh + mixed[k] * old
        total[k] = amount * fresh + total[k] * old
        top[k] = high
        return carry

    lax.fori_loop(0, kv, last_head, 0)

    for j in range(1, lines):
        to = line_at(j)
        send(answer.at[to], given.at[to], answer_send.at[to], answer_recv.at[to], peer(to, place)).wait_recv()
        send(answer_log.at[to], given_log.at[to], log_send.at[to], log_recv.at[to], peer(to, place)).wait_recv()

    square[0] = jnp.zeros_like(square[0])

    def merge_head(k, carry):
        logs = []
        high = top[k]
        for j in range(1, lines):
            log = jnp.sum(jnp.where(eye, given_log[line_at(j), k], 0.0), axis=1, keepdims=True)
            logs.append(log)
            high = jnp.maximum(high, log)
        old = jnp.exp2(top[k] - high)
        whole = mixed[k] * old
        amount = total[k] * old
        for j in range(1, lines):
            share = jnp.exp2(logs[j - 1] - high)
            whole = whole + given[line_at(j), k].astype(jnp.float32) * share
            amount = amount + share
        result = (whole / amount).astype(jnp.bfloat16)
        attn[:, :, pl.ds(k * group, group), :] = result.reshape(steps, requests, group, hdim)
        wide = result.astype(jnp.float32)
        square[0] += jnp.sum((wide * wide).reshape(groups, group, hdim), axis=1)
        return carry

    lax.fori_loop(0, kv, merge_head, 0)
    swap = send(square.at[0], square.at[1], square_sem.at[0], square_sem.at[1], {"tp": 1 - core})
    swap.start()
    swap.wait()
    mean = jnp.sum(square[0] + square[1], axis=-1, keepdims=True) / total_width
    scale = lax.rsqrt(mean + 1e-05)
    for t in range(steps):
        for g in range(requests):
            row = t * requests + g
            wide = attn[t, g].astype(jnp.float32)
            out[t, g] = (wide * scale[row : row + 1, :] * gain[...]).astype(out.dtype)

    for j in range(1, lines + 1):
        for i in range(1, plane):
            ship(j, i).wait_send()
        if j < lines:
            for copy in ask(j) + reply(j):
                copy.wait_send()


def attend(query, count, bias, gain, tiles, outgoing, cap, plane):
    steps, requests, heads, hdim = query.shape
    kv, page = tiles.shape[2:4]
    lines = outgoing.shape[0] // plane
    rows = steps * requests * heads // kv
    vmem = pl.BlockSpec(memory_space=pltpu.VMEM)
    dma = pltpu.SemaphoreType.DMA
    return pl.pallas_call(
        functools.partial(attend_kernel, cap, plane, lines, heads * hdim * lax.axis_size("tp")),
        out_shape=jax.ShapeDtypeStruct(query.shape, jnp.bfloat16),
        in_specs=[vmem] * 5 + [pl.BlockSpec(memory_space=pl.ANY)],
        out_specs=vmem,
        scratch_shapes=[
            pltpu.VMEM((lines, plane) + outgoing.shape[1:], jnp.bfloat16),
            pltpu.VMEM((lines,) + query.shape, jnp.bfloat16),
            pltpu.VMEM(count.shape, jnp.bfloat16),
            pltpu.VMEM((lines, kv, rows, hdim), jnp.bfloat16),
            pltpu.VMEM((lines, kv, 1, rows), jnp.float32),
            pltpu.VMEM((lines, kv, rows, hdim), jnp.bfloat16),
            pltpu.VMEM((lines, kv, 1, rows), jnp.float32),
            pltpu.VMEM((kv, rows, hdim), jnp.float32),
            pltpu.VMEM((kv, rows, 1), jnp.float32),
            pltpu.VMEM((kv, rows, 1), jnp.float32),
            pltpu.VMEM(query.shape, jnp.bfloat16),
            pltpu.VMEM((2, steps * requests, hdim), jnp.float32),
            dma((lines,)),
            dma((lines, plane)),
            dma((lines, plane)),
        ]
        + [dma((lines,))] * 8
        + [dma((2,))],
        compiler_params=pltpu.CompilerParams(
            vmem_limit_bytes=VMEM_LIMIT, collective_id=0, has_side_effects=True
        ),
        name="attend",
    )(query, count, bias, gain, tiles, outgoing)


def filled_tail(unfinished, fresh, fill):
    offset = jnp.arange(unfinished.shape[2], dtype=jnp.int32)[None, None, :, None, None]
    out = unfinished
    for s in range(fresh.shape[0]):
        out = jnp.where(offset == fill[:, None, None, None, None] + s, fresh[s][:, :, None], out)
    return out


def body(query, fresh, unfinished, store, table, history, fill, sender, target, switch, gain):
    replicas = lax.axis_size("rep")
    steps, requests, heads, hdim = query.shape
    cap = max(2, 2 * sender.shape[0] // replicas)
    plane = math.gcd(4, replicas)
    tiles = jnp.concatenate([store, filled_tail(unfinished, fresh, fill)], 0)
    tiles = jnp.transpose(tiles, (0, 1, 3, 2, 4))
    outgoing, count, bias = pack(
        tiles, sender, target, table, history, fill, switch, steps, replicas, cap, plane
    )
    normed = attend(query, count, bias, gain.reshape(heads, hdim), tiles, outgoing, cap, plane)
    return normed.reshape(steps, requests, heads * hdim)


def solution(mesh):
    placed = (
        P(None, "rep", "tp", None),
        P(None, "rep", None, "tp", None),
        P("rep", None, None, "tp", None),
        P("rep", None, None, "tp", None),
        P("rep", None),
        P("rep"),
        P("rep"),
        P("rep"),
        P("rep", None),
        P("rep"),
        P("tp"),
    )
    return jax.shard_map(
        body, mesh=mesh, in_specs=placed, out_specs=P(None, "rep", "tp"), check_vma=False
    )
```

```python
import functools
import math

import jax
import jax.numpy as jnp
from jax import lax
from jax.experimental import pallas as pl
from jax.experimental.pallas import tpu as pltpu
from jax.sharding import PartitionSpec as P

NEG = -1e30
LOG2E = 1.4426950408889634
VMEM_LIMIT = 50 * 1024 * 1024


def counts_of(table, history, first, pages, page):
    requests, entries = table.shape
    offset = lax.broadcasted_iota(jnp.int32, (page, entries), 0)
    position = lax.broadcasted_iota(jnp.int32, (page, entries), 1) * page + offset
    named = lax.broadcasted_iota(jnp.int32, (pages, entries), 0) + first
    per_page = []
    for g in range(requests):
        inside = jnp.where(position < history[g], 1.0, 0.0).astype(jnp.bfloat16)
        hit = jnp.where(table[g : g + 1, :] == named, 1.0, 0.0).astype(jnp.bfloat16)
        per_page.append(
            lax.dot_general(inside, hit, (((1,), (1,)), ((), ())), preferred_element_type=jnp.float32)
        )
    tokens = pages * page
    spread = (
        lax.broadcasted_iota(jnp.int32, (pages, tokens), 1) // page
        == lax.broadcasted_iota(jnp.int32, (pages, tokens), 0)
    )
    wide = jnp.dot(
        jnp.concatenate(per_page, 0).astype(jnp.bfloat16),
        jnp.where(spread, 1.0, 0.0).astype(jnp.bfloat16),
        preferred_element_type=jnp.float32,
    )
    own = (
        lax.broadcasted_iota(jnp.int32, (page, tokens), 1) % page
        == lax.broadcasted_iota(jnp.int32, (page, tokens), 0)
    )
    return [
        jnp.sum(jnp.where(own, wide[g * page : (g + 1) * page], 0.0), axis=0, keepdims=True)
        for g in range(requests)
    ]


def bias_of(count):
    return jnp.where(count > 0.0, jnp.log2(jnp.maximum(count, 1.0)), NEG)


def head_scores(query, keys, bias):
    rows, hdim = query.shape
    scores = lax.dot_general(query, keys, (((1,), (1,)), ((), ())), preferred_element_type=jnp.float32)
    groups = bias.shape[0]
    scores = scores.reshape(groups, rows // groups, -1) * (LOG2E / math.sqrt(hdim)) + bias[:, None, :]
    return scores.reshape(rows, -1)


def plan_kernel(cap, pool, sender, target, fill, switch, unfinished, fresh, source, length, tails, held):
    requests, parts, kv, page, hdim = unfinished.shape
    slots = source.shape[0]
    for s in range(slots):
        source[s] = 0
        length[s] = 0
    for d in range(slots // cap):
        held[d] = d * cap

    def place(e, carry):
        d = target[e]
        slot = held[d]
        held[d] = slot + 1
        tile = sender[e]
        owner = jnp.maximum(tile - pool, 0)
        source[slot] = tile
        length[slot] = jnp.where(tile >= pool, fill[owner] + switch[owner], page)
        return carry

    lax.fori_loop(0, target.shape[0], place, 0)
    offset = lax.broadcasted_iota(jnp.int32, (page, hdim), 0)
    for g in range(requests):
        for c in range(parts):
            steps = [fresh[s, g, c].astype(jnp.float32) for s in range(fresh.shape[0])]
            for k in range(kv):
                block = unfinished[g, c, k].astype(jnp.float32)
                for s in range(len(steps)):
                    block = jnp.where(offset == fill[g] + s, steps[s][k : k + 1, :], block)
                tails[g, c, k] = block.astype(tails.dtype)


def plan(sender, target, fill, switch, unfinished, fresh, pool, replicas, cap):
    smem = pl.BlockSpec(memory_space=pltpu.SMEM)
    vmem = pl.BlockSpec(memory_space=pltpu.VMEM)
    slots = jax.ShapeDtypeStruct((replicas * cap,), jnp.int32)
    return pl.pallas_call(
        functools.partial(plan_kernel, cap, pool),
        out_shape=(slots, slots, jax.ShapeDtypeStruct(unfinished.shape, unfinished.dtype)),
        in_specs=[smem] * 4 + [vmem] * 2,
        out_specs=(smem, smem, vmem),
        scratch_shapes=[pltpu.SMEM((replicas,), jnp.int32)],
        compiler_params=pltpu.CompilerParams(vmem_limit_bytes=VMEM_LIMIT),
        name="plan",
    )(sender, target, fill, switch, unfinished, fresh)


def partial(query, keys, values, bias):
    scores = head_scores(query, keys, bias)
    best = jnp.max(scores, axis=-1, keepdims=True)
    probs = jnp.exp2(scores - best)
    total = jnp.sum(probs, axis=-1, keepdims=True)
    return jnp.dot(probs.astype(jnp.bfloat16), values, preferred_element_type=jnp.float32), best, total


def diagonal(size):
    return lax.broadcasted_iota(jnp.int32, (size, size), 0) == lax.broadcasted_iota(jnp.int32, (size, size), 1)


def attend_kernel(
    cap, plane, lines, total_width,
    source, length, history, fill, switch,
    query, table, gain, tiles, tails,
    out,
    outgoing, count, bias, last_bias, arrived, asked, asked_count, answer, answer_log, given, given_log, mixed, top, total, attn, square,
    tile_send, tile_recv, ask_send, ask_recv, count_send, count_recv,
    answer_send, answer_recv, log_send, log_recv, square_sem,
):
    steps, requests, heads, hdim = query.shape
    pool, parts, kv, page, _ = tiles.shape
    group = heads // kv
    groups = steps * requests
    rows = groups * group
    tokens = plane * cap * page
    me = lax.axis_index("rep")
    core = lax.axis_index("tp")
    line, place = lax.div(me, plane), lax.rem(me, plane)

    def peer(a_line, a_place):
        return {"rep": a_line * plane + a_place}

    def send(source, target, send_sem, recv_sem, device):
        return pltpu.make_async_remote_copy(
            src_ref=source, dst_ref=target, send_sem=send_sem, recv_sem=recv_sem,
            device_id=device, device_id_type=pl.DeviceIdType.MESH,
        )

    def line_at(step):
        return lax.rem(line + step, lines)

    def line_back(step):
        return lax.rem(line + lines - step, lines)

    def place_at(step):
        if plane == 4:
            y, x = lax.div(place, 2), lax.rem(place, 2)
            return lax.rem(y + step // 2, 2) * 2 + lax.rem(x + step % 2, 2)
        return lax.rem(place + step, plane)

    barrier = pltpu.get_barrier_semaphore()
    for j in range(1, lines):
        pl.semaphore_signal(barrier, inc=1, device_id=peer(line_at(j), place), device_id_type=pl.DeviceIdType.MESH)
    for i in range(1, plane):
        pl.semaphore_signal(barrier, inc=1, device_id=peer(line, place_at(i)), device_id_type=pl.DeviceIdType.MESH)
    pl.semaphore_signal(barrier, inc=1, device_id={"tp": 1 - core}, device_id_type=pl.DeviceIdType.MESH)
    pl.semaphore_wait(barrier, lines + plane - 1)

    def ask(j):
        to = line_at(j)
        return send(query, asked.at[line], ask_send.at[to], ask_recv.at[line], peer(to, place))

    def ask_counts(j):
        to = line_at(j)
        return send(
            count.at[to], asked_count.at[line], count_send.at[to], count_recv.at[line], peer(to, place)
        )

    def ship(j, i):
        to = line_at(j)
        mate = place_at(i)
        return send(
            outgoing.at[to * plane + mate], arrived.at[to, place],
            tile_send.at[to, mate], tile_recv.at[to, place], peer(line, mate),
        )

    def reply(j):
        to = line_at(j)
        return (
            send(answer.at[to], given.at[line], answer_send.at[to], answer_recv.at[line], peer(to, place)),
            send(answer_log.at[to], given_log.at[line], log_send.at[to], log_recv.at[line], peer(to, place)),
        )

    lane = lax.broadcasted_iota(jnp.int32, (page, hdim), 1)

    def fill_block(block, receiver):
        def one_slot(rank, mask):
            tile = source[receiver * cap + rank]
            for c in range(parts):
                for k in range(kv):
                    block[(c * kv + k) * cap + rank] = jnp.where(
                        tile >= pool,
                        tails[jnp.maximum(tile - pool, 0), c, k],
                        tiles[jnp.minimum(tile, pool - 1), c, k],
                    )
            lo = rank * page
            return jnp.where((lane >= lo) & (lane < lo + length[receiver * cap + rank]), 1.0, mask)

        mask = lax.fori_loop(0, cap, one_slot, jnp.zeros((page, hdim), jnp.float32))
        block[parts * kv * cap] = mask.astype(jnp.bfloat16)

    order = list(range(plane - 1, 0, -1))
    for j in range(1, lines + 1):
        to = line_at(j)
        for i in order:
            receiver = to * plane + place_at(i)
            fill_block(outgoing.at[receiver], receiver)
            ship(j, i).start()
        if j < lines:
            ask(lines - j).start()
    for j in range(1, lines + 1):
        fill_block(arrived.at[line_at(j), place], line_at(j) * plane + place)

    tokens_in = counts_of(table, history, pool, lines * plane * cap, page)
    for to in range(lines):
        parts_of = [
            jnp.where(t >= switch[g], tokens_in[g][:, to * tokens : (to + 1) * tokens], 0.0)
            for t in range(steps)
            for g in range(requests)
        ]
        count[to] = jnp.concatenate(parts_of, 0).astype(count.dtype)
    for j in range(1, lines):
        ask_counts(lines - j).start()

    own = counts_of(table, history, 0, pool, page)
    tail = lax.broadcasted_iota(jnp.int32, (1, requests * page), 1)
    for t in range(steps):
        for g in range(requests):
            row = t * requests + g
            bias[row : row + 1, : pool * page] = bias_of(own[g])
            seen = (tail // page == g) & (tail % page < fill[g] + t + 1)
            bias[row : row + 1, pool * page :] = jnp.where(seen, 0.0, NEG)

    def pool_head(k, carry):
        q = query[:, :, pl.ds(k * group, group), :].reshape(rows, hdim)
        both = [
            jnp.concatenate(
                [tiles[:, c, k].reshape(pool * page, hdim), tails[:, c, k].reshape(requests * page, hdim)], 0
            )
            for c in range(2)
        ]
        mixed[k], top[k], total[k] = partial(q, both[0], both[1], bias[...])
        return carry

    lax.fori_loop(0, kv, pool_head, 0)

    width = cap * page
    repeat = (
        lax.broadcasted_iota(jnp.int32, (hdim, tokens), 1) % width
        == lax.broadcasted_iota(jnp.int32, (hdim, tokens), 0)
    )
    repeat = jnp.where(repeat, 1.0, 0.0).astype(jnp.bfloat16)
    mine = (
        lax.broadcasted_iota(jnp.int32, (plane, tokens), 1) // width
        == lax.broadcasted_iota(jnp.int32, (plane, tokens), 0)
    )
    eye = diagonal(rows)

    def ship_in(to, mate):
        return send(
            outgoing.at[to * plane + mate], arrived.at[to, mate], tile_send.at[to, mate], tile_recv.at[to, mate],
            peer(line, mate),
        )

    def filled(to):
        here = arrived[to, :, 2 * kv * cap, 0, :]
        spread = jnp.dot(here, repeat, preferred_element_type=jnp.float32)
        return jnp.sum(jnp.where(mine, spread, 0.0), axis=0, keepdims=True)

    def arrivals(to, k):
        keys = arrived[to, :, pl.ds(k * cap, cap)].reshape(tokens, hdim)
        values = arrived[to, :, pl.ds((kv + k) * cap, cap)].reshape(tokens, hdim)
        return keys, values

    for j in range(1, lines):
        to = line_at(j)
        for i in order:
            mate = place_at(i)
            ship_in(to, mate).wait_recv()
        send(query, asked.at[to], ask_send.at[to], ask_recv.at[to], peer(to, place)).wait_recv()
        send(
            count.at[to], asked_count.at[to], count_send.at[to], count_recv.at[to], peer(to, place)
        ).wait_recv()
        set_bias = bias_of(asked_count[to].astype(jnp.float32) * filled(to))

        def set_head(k, carry):
            q = asked[to, :, :, pl.ds(k * group, group), :].reshape(rows, hdim)
            keys, values = arrivals(to, k)
            part, best, amount = partial(q, keys, values, set_bias)
            answer[to, k] = (part / amount).astype(jnp.bfloat16)
            log = best + jnp.log2(amount)
            answer_log[to, k] = jnp.sum(jnp.where(eye, log, 0.0), axis=0, keepdims=True)
            return carry

        lax.fori_loop(0, kv, set_head, 0)
        for copy in reply(j):
            copy.start()

    for j in range(1, lines):
        to = line_at(j)
        send(answer.at[to], given.at[to], answer_send.at[to], answer_recv.at[to], peer(to, place)).wait_recv()
        send(answer_log.at[to], given_log.at[to], log_send.at[to], log_recv.at[to], peer(to, place)).wait_recv()

    def merge_head(k, carry):
        logs = []
        high = top[k]
        for j in range(1, lines):
            log = jnp.sum(jnp.where(eye, given_log[line_at(j), k], 0.0), axis=1, keepdims=True)
            logs.append(log)
            high = jnp.maximum(high, log)
        old = jnp.exp2(top[k] - high)
        whole = mixed[k] * old
        amount = total[k] * old
        for j in range(1, lines):
            share = jnp.exp2(logs[j - 1] - high)
            whole = whole + given[line_at(j), k].astype(jnp.float32) * share
            amount = amount + share
        mixed[k], total[k], top[k] = whole, amount, high
        return carry

    lax.fori_loop(0, kv, merge_head, 0)
    square[0] = jnp.zeros_like(square[0])

    for i in [0] + order:
        mate = place_at(i)
        if i > 0:
            ship_in(line, mate).wait_recv()
        here = arrived[line, mate, parts * kv * cap, 0:1, :].astype(jnp.float32)
        for m in range(plane):
            part = count[line, :, m * width : (m + 1) * width].astype(jnp.float32)
            mine_count = part if m == 0 else jnp.where(mate == m, part, mine_count)
        last_bias[...] = bias_of(mine_count * here[:, :width])

        def last_head(k, carry, mate=mate, last=i == order[-1]):
            q = query[:, :, pl.ds(k * group, group), :].reshape(rows, hdim)
            keys = arrived[line, mate, pl.ds(k * cap, cap)].reshape(width, hdim)
            values = arrived[line, mate, pl.ds((kv + k) * cap, cap)].reshape(width, hdim)
            part, best, amount = partial(q, keys, values, last_bias[...])
            high = jnp.maximum(best, top[k])
            fresh, old = jnp.exp2(best - high), jnp.exp2(top[k] - high)
            whole = part * fresh + mixed[k] * old
            amount = amount * fresh + total[k] * old
            if not last:
                mixed[k], total[k], top[k] = whole, amount, high
                return carry
            result = (whole / amount).astype(jnp.bfloat16)
            attn[:, :, pl.ds(k * group, group), :] = result.reshape(steps, requests, group, hdim)
            wide = result.astype(jnp.float32)
            square[0] += jnp.sum((wide * wide).reshape(groups, group, hdim), axis=1)
            return carry

        lax.fori_loop(0, kv, last_head, 0)

    swap = send(square.at[0], square.at[1], square_sem.at[0], square_sem.at[1], {"tp": 1 - core})
    swap.start()
    swap.wait()
    mean = jnp.sum(square[0] + square[1], axis=-1, keepdims=True) / total_width
    scale = lax.rsqrt(mean + 1e-05)
    for t in range(steps):
        for g in range(requests):
            row = t * requests + g
            wide = attn[t, g].astype(jnp.float32)
            out[t, g] = (wide * scale[row : row + 1, :] * gain[...]).astype(out.dtype)

    for j in range(1, lines + 1):
        for i in range(1, plane):
            ship(j, i).wait_send()
        if j < lines:
            for copy in (ask(j), ask_counts(j)) + reply(j):
                copy.wait_send()


def attend(source, length, history, fill, switch, query, table, gain, tiles, tails, cap, plane, lines):
    steps, requests, heads, hdim = query.shape
    pool, parts, kv, page, _ = tiles.shape
    rows = steps * requests * heads // kv
    width = cap * page
    smem = pl.BlockSpec(memory_space=pltpu.SMEM)
    vmem = pl.BlockSpec(memory_space=pltpu.VMEM)
    dma = pltpu.SemaphoreType.DMA
    block = (parts * kv * cap + 1, page, hdim)
    return pl.pallas_call(
        functools.partial(attend_kernel, cap, plane, lines, heads * hdim * lax.axis_size("tp")),
        out_shape=jax.ShapeDtypeStruct(query.shape, jnp.bfloat16),
        in_specs=[smem] * 5 + [vmem] * 5,
        out_specs=vmem,
        scratch_shapes=[
            pltpu.VMEM((lines * plane,) + block, jnp.bfloat16),
            pltpu.VMEM((lines, steps * requests, plane * width), jnp.bfloat16),
            pltpu.VMEM((steps * requests, (pool + requests) * page), jnp.float32),
            pltpu.VMEM((steps * requests, width), jnp.float32),
            pltpu.VMEM((lines, plane) + block, jnp.bfloat16),
            pltpu.VMEM((lines,) + query.shape, jnp.bfloat16),
            pltpu.VMEM((lines, steps * requests, plane * width), jnp.bfloat16),
            pltpu.VMEM((lines, kv, rows, hdim), jnp.bfloat16),
            pltpu.VMEM((lines, kv, 1, rows), jnp.float32),
            pltpu.VMEM((lines, kv, rows, hdim), jnp.bfloat16),
            pltpu.VMEM((lines, kv, 1, rows), jnp.float32),
            pltpu.VMEM((kv, rows, hdim), jnp.float32),
            pltpu.VMEM((kv, rows, 1), jnp.float32),
            pltpu.VMEM((kv, rows, 1), jnp.float32),
            pltpu.VMEM(query.shape, jnp.bfloat16),
            pltpu.VMEM((2, steps * requests, hdim), jnp.float32),
            dma((lines, plane)),
            dma((lines, plane)),
        ]
        + [dma((lines,))] * 8
        + [dma((2,))],
        compiler_params=pltpu.CompilerParams(
            vmem_limit_bytes=VMEM_LIMIT, collective_id=0, has_side_effects=True
        ),
        name="attend",
    )(source, length, history, fill, switch, query, table, gain, tiles, tails)


def body(query, fresh, unfinished, store, table, history, fill, sender, target, switch, gain):
    replicas = lax.axis_size("rep")
    steps, requests, heads, hdim = query.shape
    cap = max(2, 2 * sender.shape[0] // replicas)
    plane = math.gcd(4, replicas)
    tiles = jnp.transpose(store, (0, 1, 3, 2, 4))
    source, length, tails = plan(
        sender, target.reshape(-1), fill, switch, jnp.transpose(unfinished, (0, 1, 3, 2, 4)), fresh,
        store.shape[0], replicas, cap,
    )
    normed = attend(
        source, length, history, fill, switch, query, table, gain.reshape(heads, hdim), tiles, tails,
        cap, plane, replicas // plane,
    )
    return normed.reshape(steps, requests, heads * hdim)


def solution(mesh):
    placed = (
        P(None, "rep", "tp", None),
        P(None, "rep", None, "tp", None),
        P("rep", None, None, "tp", None),
        P("rep", None, None, "tp", None),
        P("rep", None),
        P("rep"),
        P("rep"),
        P("rep"),
        P("rep", None),
        P("rep"),
        P("tp"),
    )
    return jax.shard_map(
        body, mesh=mesh, in_specs=placed, out_specs=P(None, "rep", "tp"), check_vma=False
    )
```

```python
import functools
import math

import jax
import jax.numpy as jnp
from jax import lax
from jax.experimental import pallas as pl
from jax.experimental.pallas import tpu as pltpu
from jax.sharding import PartitionSpec as P

NEG = -1e30
LOG2E = 1.4426950408889634
VMEM_LIMIT = 50 * 1024 * 1024


def counts_of(table, history, first, pages, page):
    requests, entries = table.shape
    offset = lax.broadcasted_iota(jnp.int32, (page, entries), 0)
    position = lax.broadcasted_iota(jnp.int32, (page, entries), 1) * page + offset
    named = lax.broadcasted_iota(jnp.int32, (pages, entries), 0) + first
    per_page = []
    for g in range(requests):
        inside = jnp.where(position < history[g], 1.0, 0.0).astype(jnp.bfloat16)
        hit = jnp.where(table[g : g + 1, :] == named, 1.0, 0.0).astype(jnp.bfloat16)
        per_page.append(
            lax.dot_general(inside, hit, (((1,), (1,)), ((), ())), preferred_element_type=jnp.float32)
        )
    tokens = pages * page
    spread = (
        lax.broadcasted_iota(jnp.int32, (pages, tokens), 1) // page
        == lax.broadcasted_iota(jnp.int32, (pages, tokens), 0)
    )
    wide = jnp.dot(
        jnp.concatenate(per_page, 0).astype(jnp.bfloat16),
        jnp.where(spread, 1.0, 0.0).astype(jnp.bfloat16),
        preferred_element_type=jnp.float32,
    )
    own = (
        lax.broadcasted_iota(jnp.int32, (page, tokens), 1) % page
        == lax.broadcasted_iota(jnp.int32, (page, tokens), 0)
    )
    return [
        jnp.sum(jnp.where(own, wide[g * page : (g + 1) * page], 0.0), axis=0, keepdims=True)
        for g in range(requests)
    ]


def bias_of(count):
    return jnp.where(count > 0.0, jnp.log2(jnp.maximum(count, 1.0)), NEG)


def head_scores(query, keys, bias):
    rows, hdim = query.shape
    scores = lax.dot_general(query, keys, (((1,), (1,)), ((), ())), preferred_element_type=jnp.float32)
    groups = bias.shape[0]
    scores = scores.reshape(groups, rows // groups, -1) * (LOG2E / math.sqrt(hdim)) + bias[:, None, :]
    return scores.reshape(rows, -1)


def plan_kernel(cap, sender, target, fill, switch, unfinished, fresh, tiles, source, length, tails, held):
    requests, parts, kv, page, hdim = unfinished.shape
    slots = source.shape[0]
    pool = tiles.shape[0]
    for s in range(slots):
        source[s] = 0
        length[s] = 0
    for d in range(slots // cap):
        held[d] = d * cap

    def place(e, carry):
        d = target[e]
        slot = held[d]
        held[d] = slot + 1
        tile = sender[e]
        owner = jnp.maximum(tile - pool, 0)
        source[slot] = tile
        length[slot] = jnp.where(tile >= pool, fill[owner] + switch[owner], page)
        return carry

    lax.fori_loop(0, target.shape[0], place, 0)
    offset = lax.broadcasted_iota(jnp.int32, (page, hdim), 0)
    for g in range(requests):
        for c in range(parts):
            steps = [fresh[s, g, c].astype(jnp.float32) for s in range(fresh.shape[0])]
            for k in range(kv):
                block = unfinished[g, c, k].astype(jnp.float32)
                for s in range(len(steps)):
                    block = jnp.where(offset == fill[g] + s, steps[s][k : k + 1, :], block)
                tails[g, c, k] = block.astype(tails.dtype)


def plan(sender, target, fill, switch, unfinished, fresh, tiles, replicas, cap):
    smem = pl.BlockSpec(memory_space=pltpu.SMEM)
    vmem = pl.BlockSpec(memory_space=pltpu.VMEM)
    slots = jax.ShapeDtypeStruct((replicas * cap,), jnp.int32)
    return pl.pallas_call(
        functools.partial(plan_kernel, cap),
        out_shape=(slots, slots, jax.ShapeDtypeStruct(unfinished.shape, unfinished.dtype)),
        in_specs=[smem] * 4 + [vmem] * 2 + [pl.BlockSpec(memory_space=pl.ANY)],
        out_specs=(smem, smem, vmem),
        scratch_shapes=[pltpu.SMEM((replicas,), jnp.int32)],
        compiler_params=pltpu.CompilerParams(vmem_limit_bytes=VMEM_LIMIT),
        name="plan",
    )(sender, target, fill, switch, unfinished, fresh, tiles)


def partial(query, keys, values, bias):
    scores = head_scores(query, keys, bias)
    best = jnp.max(scores, axis=-1, keepdims=True)
    probs = jnp.exp2(scores - best)
    total = jnp.sum(probs, axis=-1, keepdims=True)
    return jnp.dot(probs.astype(jnp.bfloat16), values, preferred_element_type=jnp.float32), best, total


def diagonal(size):
    return lax.broadcasted_iota(jnp.int32, (size, size), 0) == lax.broadcasted_iota(jnp.int32, (size, size), 1)


def attend_kernel(
    cap, plane, lines, total_width,
    source, length, history, fill, switch,
    query, table, gain, tiles, tails,
    out,
    outgoing, count, bias, last_bias, arrived, asked, asked_count, answer, answer_log, given, given_log, mixed, top, total, attn, square,
    tile_send, tile_recv, ask_send, ask_recv, count_send, count_recv,
    answer_send, answer_recv, log_send, log_recv, square_sem,
):
    steps, requests, heads, hdim = query.shape
    pool, parts, kv, page, _ = tiles.shape
    group = heads // kv
    groups = steps * requests
    rows = groups * group
    tokens = plane * cap * page
    me = lax.axis_index("rep")
    core = lax.axis_index("tp")
    line, place = lax.div(me, plane), lax.rem(me, plane)

    def peer(a_line, a_place):
        return {"rep": a_line * plane + a_place}

    def send(source, target, send_sem, recv_sem, device):
        return pltpu.make_async_remote_copy(
            src_ref=source, dst_ref=target, send_sem=send_sem, recv_sem=recv_sem,
            device_id=device, device_id_type=pl.DeviceIdType.MESH,
        )

    def line_at(step):
        return lax.rem(line + step, lines)

    def line_back(step):
        return lax.rem(line + lines - step, lines)

    def place_at(step):
        if plane == 4:
            if step in (1, 2):
                step = step + core * (3 - 2 * step)
            y, x = lax.div(place, 2), lax.rem(place, 2)
            return lax.rem(y + step // 2, 2) * 2 + lax.rem(x + step % 2, 2)
        return lax.rem(place + step, plane)

    barrier = pltpu.get_barrier_semaphore()
    for j in range(1, lines):
        pl.semaphore_signal(barrier, inc=1, device_id=peer(line_at(j), place), device_id_type=pl.DeviceIdType.MESH)
    for i in range(1, plane):
        pl.semaphore_signal(barrier, inc=1, device_id=peer(line, place_at(i)), device_id_type=pl.DeviceIdType.MESH)
    pl.semaphore_signal(barrier, inc=1, device_id={"tp": 1 - core}, device_id_type=pl.DeviceIdType.MESH)
    pl.semaphore_wait(barrier, lines + plane - 1)

    def ask(j):
        to = line_at(j)
        return send(query, asked.at[line], ask_send.at[to], ask_recv.at[line], peer(to, place))

    def ask_counts(j):
        to = line_at(j)
        return send(
            count.at[to], asked_count.at[line], count_send.at[to], count_recv.at[line], peer(to, place)
        )

    def ship(j, i):
        to = line_at(j)
        mate = place_at(i)
        return send(
            outgoing.at[to * plane + mate], arrived.at[to, place],
            tile_send.at[to, mate], tile_recv.at[to, place], peer(line, mate),
        )

    def reply(j):
        to = line_at(j)
        return (
            send(answer.at[to], given.at[line], answer_send.at[to], answer_recv.at[line], peer(to, place)),
            send(answer_log.at[to], given_log.at[line], log_send.at[to], log_recv.at[line], peer(to, place)),
        )

    lane = lax.broadcasted_iota(jnp.int32, (page, hdim), 1)

    def fill_block(block, receiver):
        def one_slot(rank, mask):
            tile = source[receiver * cap + rank]
            for c in range(parts):
                for k in range(kv):
                    block[(c * kv + k) * cap + rank] = jnp.where(
                        tile >= pool,
                        tails[jnp.maximum(tile - pool, 0), c, k],
                        tiles[jnp.minimum(tile, pool - 1), c, k],
                    )
            lo = rank * page
            return jnp.where((lane >= lo) & (lane < lo + length[receiver * cap + rank]), 1.0, mask)

        mask = lax.fori_loop(0, cap, one_slot, jnp.zeros((page, hdim), jnp.float32))
        block[parts * kv * cap] = mask.astype(jnp.bfloat16)

    order = list(range(1, plane))
    for j in range(1, lines + 1):
        to = line_at(j)
        for i in order:
            receiver = to * plane + place_at(i)
            fill_block(outgoing.at[receiver], receiver)
            ship(j, i).start()
        if j < lines:
            ask(lines - j).start()
    for j in range(1, lines + 1):
        fill_block(arrived.at[line_at(j), place], line_at(j) * plane + place)

    tokens_in = counts_of(table, history, pool, lines * plane * cap, page)
    for to in range(lines):
        parts_of = [
            jnp.where(t >= switch[g], tokens_in[g][:, to * tokens : (to + 1) * tokens], 0.0)
            for t in range(steps)
            for g in range(requests)
        ]
        count[to] = jnp.concatenate(parts_of, 0).astype(count.dtype)
    for j in range(1, lines):
        ask_counts(lines - j).start()

    own = counts_of(table, history, 0, pool, page)
    tail = lax.broadcasted_iota(jnp.int32, (1, requests * page), 1)
    for t in range(steps):
        for g in range(requests):
            row = t * requests + g
            bias[row : row + 1, : pool * page] = bias_of(own[g])
            seen = (tail // page == g) & (tail % page < fill[g] + t + 1)
            bias[row : row + 1, pool * page :] = jnp.where(seen, 0.0, NEG)

    def pool_head(k, carry):
        q = query[:, :, pl.ds(k * group, group), :].reshape(rows, hdim)
        both = [
            jnp.concatenate(
                [tiles[:, c, k].reshape(pool * page, hdim), tails[:, c, k].reshape(requests * page, hdim)], 0
            )
            for c in range(2)
        ]
        mixed[k], top[k], total[k] = partial(q, both[0], both[1], bias[...])
        return carry

    lax.fori_loop(0, kv, pool_head, 0)

    width = cap * page
    repeat = (
        lax.broadcasted_iota(jnp.int32, (hdim, tokens), 1) % width
        == lax.broadcasted_iota(jnp.int32, (hdim, tokens), 0)
    )
    repeat = jnp.where(repeat, 1.0, 0.0).astype(jnp.bfloat16)
    mine = (
        lax.broadcasted_iota(jnp.int32, (plane, tokens), 1) // width
        == lax.broadcasted_iota(jnp.int32, (plane, tokens), 0)
    )
    eye = diagonal(rows)

    def ship_in(to, mate):
        return send(
            outgoing.at[to * plane + mate], arrived.at[to, mate], tile_send.at[to, mate], tile_recv.at[to, mate],
            peer(line, mate),
        )

    def filled(to):
        here = arrived[to, :, 2 * kv * cap, 0, :]
        spread = jnp.dot(here, repeat, preferred_element_type=jnp.float32)
        return jnp.sum(jnp.where(mine, spread, 0.0), axis=0, keepdims=True)

    def arrivals(to, k):
        keys = arrived[to, :, pl.ds(k * cap, cap)].reshape(tokens, hdim)
        values = arrived[to, :, pl.ds((kv + k) * cap, cap)].reshape(tokens, hdim)
        return keys, values

    for j in range(1, lines):
        to = line_at(j)
        for i in order:
            mate = place_at(i)
            ship_in(to, mate).wait_recv()
        send(query, asked.at[to], ask_send.at[to], ask_recv.at[to], peer(to, place)).wait_recv()
        send(
            count.at[to], asked_count.at[to], count_send.at[to], count_recv.at[to], peer(to, place)
        ).wait_recv()
        set_bias = bias_of(asked_count[to].astype(jnp.float32) * filled(to))

        def set_head(k, carry):
            q = asked[to, :, :, pl.ds(k * group, group), :].reshape(rows, hdim)
            keys, values = arrivals(to, k)
            part, best, amount = partial(q, keys, values, set_bias)
            answer[to, k] = (part / amount).astype(jnp.bfloat16)
            log = best + jnp.log2(amount)
            answer_log[to, k] = jnp.sum(jnp.where(eye, log, 0.0), axis=0, keepdims=True)
            return carry

        lax.fori_loop(0, kv, set_head, 0)
        for copy in reply(j):
            copy.start()

    for j in range(1, lines):
        to = line_at(j)
        send(answer.at[to], given.at[to], answer_send.at[to], answer_recv.at[to], peer(to, place)).wait_recv()
        send(answer_log.at[to], given_log.at[to], log_send.at[to], log_recv.at[to], peer(to, place)).wait_recv()

    def merge_head(k, carry):
        logs = []
        high = top[k]
        for j in range(1, lines):
            log = jnp.sum(jnp.where(eye, given_log[line_at(j), k], 0.0), axis=1, keepdims=True)
            logs.append(log)
            high = jnp.maximum(high, log)
        old = jnp.exp2(top[k] - high)
        whole = mixed[k] * old
        amount = total[k] * old
        for j in range(1, lines):
            share = jnp.exp2(logs[j - 1] - high)
            whole = whole + given[line_at(j), k].astype(jnp.float32) * share
            amount = amount + share
        mixed[k], total[k], top[k] = whole, amount, high
        return carry

    lax.fori_loop(0, kv, merge_head, 0)
    square[0] = jnp.zeros_like(square[0])

    for i in [0] + order:
        mate = place_at(i)
        if i > 0:
            ship_in(line, mate).wait_recv()
        here = arrived[line, mate, parts * kv * cap, 0:1, :].astype(jnp.float32)
        for m in range(plane):
            part = count[line, :, m * width : (m + 1) * width].astype(jnp.float32)
            mine_count = part if m == 0 else jnp.where(mate == m, part, mine_count)
        last_bias[...] = bias_of(mine_count * here[:, :width])

        def last_head(k, carry, mate=mate, last=i == order[-1]):
            q = query[:, :, pl.ds(k * group, group), :].reshape(rows, hdim)
            keys = arrived[line, mate, pl.ds(k * cap, cap)].reshape(width, hdim)
            values = arrived[line, mate, pl.ds((kv + k) * cap, cap)].reshape(width, hdim)
            part, best, amount = partial(q, keys, values, last_bias[...])
            high = jnp.maximum(best, top[k])
            fresh, old = jnp.exp2(best - high), jnp.exp2(top[k] - high)
            whole = part * fresh + mixed[k] * old
            amount = amount * fresh + total[k] * old
            if not last:
                mixed[k], total[k], top[k] = whole, amount, high
                return carry
            result = (whole / amount).astype(jnp.bfloat16)
            attn[:, :, pl.ds(k * group, group), :] = result.reshape(steps, requests, group, hdim)
            wide = result.astype(jnp.float32)
            square[0] += jnp.sum((wide * wide).reshape(groups, group, hdim), axis=1)
            return carry

        lax.fori_loop(0, kv, last_head, 0)

    swap = send(square.at[0], square.at[1], square_sem.at[0], square_sem.at[1], {"tp": 1 - core})
    swap.start()
    swap.wait()
    mean = jnp.sum(square[0] + square[1], axis=-1, keepdims=True) / total_width
    scale = lax.rsqrt(mean + 1e-05)
    for t in range(steps):
        for g in range(requests):
            row = t * requests + g
            wide = attn[t, g].astype(jnp.float32)
            out[t, g] = (wide * scale[row : row + 1, :] * gain[...]).astype(out.dtype)

    for j in range(1, lines + 1):
        for i in range(1, plane):
            ship(j, i).wait_send()
        if j < lines:
            for copy in (ask(j), ask_counts(j)) + reply(j):
                copy.wait_send()


def attend(source, length, history, fill, switch, query, table, gain, tiles, tails, cap, plane, lines):
    steps, requests, heads, hdim = query.shape
    pool, parts, kv, page, _ = tiles.shape
    rows = steps * requests * heads // kv
    width = cap * page
    smem = pl.BlockSpec(memory_space=pltpu.SMEM)
    vmem = pl.BlockSpec(memory_space=pltpu.VMEM)
    dma = pltpu.SemaphoreType.DMA
    block = (parts * kv * cap + 1, page, hdim)
    return pl.pallas_call(
        functools.partial(attend_kernel, cap, plane, lines, heads * hdim * lax.axis_size("tp")),
        out_shape=jax.ShapeDtypeStruct(query.shape, jnp.bfloat16),
        in_specs=[smem] * 5 + [vmem] * 5,
        out_specs=vmem,
        scratch_shapes=[
            pltpu.VMEM((lines * plane,) + block, jnp.bfloat16),
            pltpu.VMEM((lines, steps * requests, plane * width), jnp.bfloat16),
            pltpu.VMEM((steps * requests, (pool + requests) * page), jnp.float32),
            pltpu.VMEM((steps * requests, width), jnp.float32),
            pltpu.VMEM((lines, plane) + block, jnp.bfloat16),
            pltpu.VMEM((lines,) + query.shape, jnp.bfloat16),
            pltpu.VMEM((lines, steps * requests, plane * width), jnp.bfloat16),
            pltpu.VMEM((lines, kv, rows, hdim), jnp.bfloat16),
            pltpu.VMEM((lines, kv, 1, rows), jnp.float32),
            pltpu.VMEM((lines, kv, rows, hdim), jnp.bfloat16),
            pltpu.VMEM((lines, kv, 1, rows), jnp.float32),
            pltpu.VMEM((kv, rows, hdim), jnp.float32),
            pltpu.VMEM((kv, rows, 1), jnp.float32),
            pltpu.VMEM((kv, rows, 1), jnp.float32),
            pltpu.VMEM(query.shape, jnp.bfloat16),
            pltpu.VMEM((2, steps * requests, hdim), jnp.float32),
            dma((lines, plane)),
            dma((lines, plane)),
        ]
        + [dma((lines,))] * 8
        + [dma((2,))],
        compiler_params=pltpu.CompilerParams(
            vmem_limit_bytes=VMEM_LIMIT, collective_id=0, has_side_effects=True
        ),
        name="attend",
    )(source, length, history, fill, switch, query, table, gain, tiles, tails)


def body(query, fresh, unfinished, store, table, history, fill, sender, target, switch, gain):
    replicas = lax.axis_size("rep")
    steps, requests, heads, hdim = query.shape
    cap = max(2, 2 * sender.shape[0] // replicas)
    plane = math.gcd(4, replicas)
    tiles = jnp.transpose(store, (0, 1, 3, 2, 4))
    source, length, tails = plan(
        sender, target.reshape(-1), fill, switch, jnp.transpose(unfinished, (0, 1, 3, 2, 4)), fresh,
        tiles, replicas, cap,
    )
    normed = attend(
        source, length, history, fill, switch, query, table, gain.reshape(heads, hdim), tiles, tails,
        cap, plane, replicas // plane,
    )
    return normed.reshape(steps, requests, heads * hdim)


def solution(mesh):
    placed = (
        P(None, "rep", "tp", None),
        P(None, "rep", None, "tp", None),
        P("rep", None, None, "tp", None),
        P("rep", None, None, "tp", None),
        P("rep", None),
        P("rep"),
        P("rep"),
        P("rep"),
        P("rep", None),
        P("rep"),
        P("tp"),
    )
    return jax.shard_map(
        body, mesh=mesh, in_specs=placed, out_specs=P(None, "rep", "tp"), check_vma=False
    )
```

```python
import functools
import math

import jax
import jax.numpy as jnp
from jax import lax
from jax.experimental import pallas as pl
from jax.experimental.pallas import tpu as pltpu
from jax.sharding import PartitionSpec as P

NEG = -1e30
LOG2E = 1.4426950408889634
VMEM_LIMIT = 50 * 1024 * 1024


def counts_of(table, history, first, pages, page):
    requests, entries = table.shape
    offset = lax.broadcasted_iota(jnp.int32, (page, entries), 0)
    position = lax.broadcasted_iota(jnp.int32, (page, entries), 1) * page + offset
    named = lax.broadcasted_iota(jnp.int32, (pages, entries), 0) + first
    per_page = []
    for g in range(requests):
        inside = jnp.where(position < history[g], 1.0, 0.0).astype(jnp.bfloat16)
        hit = jnp.where(table[g : g + 1, :] == named, 1.0, 0.0).astype(jnp.bfloat16)
        per_page.append(
            lax.dot_general(inside, hit, (((1,), (1,)), ((), ())), preferred_element_type=jnp.float32)
        )
    tokens = pages * page
    spread = (
        lax.broadcasted_iota(jnp.int32, (pages, tokens), 1) // page
        == lax.broadcasted_iota(jnp.int32, (pages, tokens), 0)
    )
    wide = jnp.dot(
        jnp.concatenate(per_page, 0).astype(jnp.bfloat16),
        jnp.where(spread, 1.0, 0.0).astype(jnp.bfloat16),
        preferred_element_type=jnp.float32,
    )
    own = (
        lax.broadcasted_iota(jnp.int32, (page, tokens), 1) % page
        == lax.broadcasted_iota(jnp.int32, (page, tokens), 0)
    )
    return [
        jnp.sum(jnp.where(own, wide[g * page : (g + 1) * page], 0.0), axis=0, keepdims=True)
        for g in range(requests)
    ]


def bias_of(count):
    return jnp.where(count > 0.0, jnp.log2(jnp.maximum(count, 1.0)), NEG)


def head_scores(query, keys, bias):
    rows, hdim = query.shape
    scores = lax.dot_general(query, keys, (((1,), (1,)), ((), ())), preferred_element_type=jnp.float32)
    groups = bias.shape[0]
    scores = scores.reshape(groups, rows // groups, -1) * (LOG2E / math.sqrt(hdim)) + bias[:, None, :]
    return scores.reshape(rows, -1)


def plan_kernel(cap, sender, target, fill, switch, unfinished, fresh, tiles, source, length, tails, held):
    requests, parts, kv, page, hdim = unfinished.shape
    slots = source.shape[0]
    pool = tiles.shape[0]
    for s in range(slots):
        source[s] = 0
        length[s] = 0
    for d in range(slots // cap):
        held[d] = d * cap

    def place(e, carry):
        d = target[e]
        slot = held[d]
        held[d] = slot + 1
        tile = sender[e]
        owner = jnp.maximum(tile - pool, 0)
        source[slot] = tile
        length[slot] = jnp.where(tile >= pool, fill[owner] + switch[owner], page)
        return carry

    lax.fori_loop(0, target.shape[0], place, 0)
    offset = lax.broadcasted_iota(jnp.int32, (page, hdim), 0)
    for g in range(requests):
        for c in range(parts):
            steps = [fresh[s, g, c].astype(jnp.float32) for s in range(fresh.shape[0])]
            for k in range(kv):
                block = unfinished[g, c, k].astype(jnp.float32)
                for s in range(len(steps)):
                    block = jnp.where(offset == fill[g] + s, steps[s][k : k + 1, :], block)
                tails[g, c, k] = block.astype(tails.dtype)


def plan(sender, target, fill, switch, unfinished, fresh, tiles, replicas, cap):
    smem = pl.BlockSpec(memory_space=pltpu.SMEM)
    vmem = pl.BlockSpec(memory_space=pltpu.VMEM)
    slots = jax.ShapeDtypeStruct((replicas * cap,), jnp.int32)
    return pl.pallas_call(
        functools.partial(plan_kernel, cap),
        out_shape=(slots, slots, jax.ShapeDtypeStruct(unfinished.shape, unfinished.dtype)),
        in_specs=[smem] * 4 + [vmem] * 2 + [pl.BlockSpec(memory_space=pl.ANY)],
        out_specs=(smem, smem, vmem),
        scratch_shapes=[pltpu.SMEM((replicas,), jnp.int32)],
        compiler_params=pltpu.CompilerParams(vmem_limit_bytes=VMEM_LIMIT),
        name="plan",
    )(sender, target, fill, switch, unfinished, fresh, tiles)


def partial(query, keys, values, bias):
    scores = head_scores(query, keys, bias)
    best = jnp.max(scores, axis=-1, keepdims=True)
    probs = jnp.exp2(scores - best)
    total = jnp.sum(probs, axis=-1, keepdims=True)
    return jnp.dot(probs.astype(jnp.bfloat16), values, preferred_element_type=jnp.float32), best, total


def diagonal(size):
    return lax.broadcasted_iota(jnp.int32, (size, size), 0) == lax.broadcasted_iota(jnp.int32, (size, size), 1)


def attend_kernel(
    cap, plane, lines, total_width,
    source, length, history, fill, switch,
    query, table, gain, tiles, tails,
    out,
    outgoing, count, bias, last_bias, arrived, asked, asked_count, answer, answer_log, given, given_log, mixed, top, total, attn, square,
    tile_send, tile_recv, ask_send, ask_recv, count_send, count_recv,
    answer_send, answer_recv, log_send, log_recv, square_sem,
):
    steps, requests, heads, hdim = query.shape
    pool, parts, kv, page, _ = tiles.shape
    group = heads // kv
    groups = steps * requests
    rows = groups * group
    tokens = plane * cap * page
    me = lax.axis_index("rep")
    core = lax.axis_index("tp")
    line, place = lax.div(me, plane), lax.rem(me, plane)

    def peer(a_line, a_place):
        return {"rep": a_line * plane + a_place}

    def send(source, target, send_sem, recv_sem, device):
        return pltpu.make_async_remote_copy(
            src_ref=source, dst_ref=target, send_sem=send_sem, recv_sem=recv_sem,
            device_id=device, device_id_type=pl.DeviceIdType.MESH,
        )

    def line_at(step):
        return lax.rem(line + step, lines)

    def line_back(step):
        return lax.rem(line + lines - step, lines)

    def place_at(step):
        if plane == 4:
            if step in (1, 2):
                step = step + core * (3 - 2 * step)
            y, x = lax.div(place, 2), lax.rem(place, 2)
            return lax.rem(y + step // 2, 2) * 2 + lax.rem(x + step % 2, 2)
        return lax.rem(place + step, plane)

    barrier = pltpu.get_barrier_semaphore()
    for j in range(1, lines):
        pl.semaphore_signal(barrier, inc=1, device_id=peer(line_at(j), place), device_id_type=pl.DeviceIdType.MESH)
    for i in range(1, plane):
        pl.semaphore_signal(barrier, inc=1, device_id=peer(line, place_at(i)), device_id_type=pl.DeviceIdType.MESH)
    pl.semaphore_signal(barrier, inc=1, device_id={"tp": 1 - core}, device_id_type=pl.DeviceIdType.MESH)
    pl.semaphore_wait(barrier, lines + plane - 1)

    def ask(j):
        to = line_at(j)
        return send(query, asked.at[line], ask_send.at[to], ask_recv.at[line], peer(to, place))

    def ask_counts(j):
        to = line_at(j)
        return send(
            count.at[to], asked_count.at[line], count_send.at[to], count_recv.at[line], peer(to, place)
        )

    def ship(j, i):
        to = line_at(j)
        mate = place_at(i)
        return send(
            outgoing.at[to * plane + mate], arrived.at[to, place],
            tile_send.at[to, mate], tile_recv.at[to, place], peer(line, mate),
        )

    def reply(j):
        to = line_at(j)
        return (
            send(answer.at[to], given.at[line], answer_send.at[to], answer_recv.at[line], peer(to, place)),
            send(answer_log.at[to], given_log.at[line], log_send.at[to], log_recv.at[line], peer(to, place)),
        )

    lane = lax.broadcasted_iota(jnp.int32, (page, hdim), 1)

    def fill_block(block, receiver):
        def one_slot(rank, mask):
            tile = source[receiver * cap + rank]
            for c in range(parts):
                for k in range(kv):
                    block[(c * kv + k) * cap + rank] = jnp.where(
                        tile >= pool,
                        tails[jnp.maximum(tile - pool, 0), c, k],
                        tiles[jnp.minimum(tile, pool - 1), c, k],
                    )
            lo = rank * page
            return jnp.where((lane >= lo) & (lane < lo + length[receiver * cap + rank]), 1.0, mask)

        mask = lax.fori_loop(0, cap, one_slot, jnp.zeros((page, hdim), jnp.float32))
        block[parts * kv * cap] = mask.astype(jnp.bfloat16)

    order = list(range(1, plane))

    def launch(j, pieces):
        for i in pieces:
            receiver = line_at(j) * plane + place_at(i)
            fill_block(outgoing.at[receiver], receiver)
            ship(j, i).start()

    launch(1, order[:1])
    tokens_in = counts_of(table, history, pool, lines * plane * cap, page)
    for to in range(lines):
        parts_of = [
            jnp.where(t >= switch[g], tokens_in[g][:, to * tokens : (to + 1) * tokens], 0.0)
            for t in range(steps)
            for g in range(requests)
        ]
        count[to] = jnp.concatenate(parts_of, 0).astype(count.dtype)
    if lines > 1:
        ask(lines - 1).start()
        ask_counts(lines - 1).start()
    launch(1, order[1:])
    for j in range(2, lines):
        ask(lines - j).start()
        ask_counts(lines - j).start()
    if lines > 1:
        launch(2, order[:1])
    for j in range(1, lines + 1):
        fill_block(arrived.at[line_at(j), place], line_at(j) * plane + place)

    own = counts_of(table, history, 0, pool, page)
    tail = lax.broadcasted_iota(jnp.int32, (1, requests * page), 1)
    for t in range(steps):
        for g in range(requests):
            row = t * requests + g
            bias[row : row + 1, : pool * page] = bias_of(own[g])
            seen = (tail // page == g) & (tail % page < fill[g] + t + 1)
            bias[row : row + 1, pool * page :] = jnp.where(seen, 0.0, NEG)

    def pool_head(k, carry):
        q = query[:, :, pl.ds(k * group, group), :].reshape(rows, hdim)
        both = [
            jnp.concatenate(
                [tiles[:, c, k].reshape(pool * page, hdim), tails[:, c, k].reshape(requests * page, hdim)], 0
            )
            for c in range(2)
        ]
        mixed[k], top[k], total[k] = partial(q, both[0], both[1], bias[...])
        return carry

    lax.fori_loop(0, kv, pool_head, 0)

    width = cap * page
    repeat = (
        lax.broadcasted_iota(jnp.int32, (hdim, tokens), 1) % width
        == lax.broadcasted_iota(jnp.int32, (hdim, tokens), 0)
    )
    repeat = jnp.where(repeat, 1.0, 0.0).astype(jnp.bfloat16)
    mine = (
        lax.broadcasted_iota(jnp.int32, (plane, tokens), 1) // width
        == lax.broadcasted_iota(jnp.int32, (plane, tokens), 0)
    )
    eye = diagonal(rows)

    def ship_in(to, mate):
        return send(
            outgoing.at[to * plane + mate], arrived.at[to, mate], tile_send.at[to, mate], tile_recv.at[to, mate],
            peer(line, mate),
        )

    def filled(to):
        here = arrived[to, :, 2 * kv * cap, 0, :]
        spread = jnp.dot(here, repeat, preferred_element_type=jnp.float32)
        return jnp.sum(jnp.where(mine, spread, 0.0), axis=0, keepdims=True)

    def arrivals(to, k):
        keys = arrived[to, :, pl.ds(k * cap, cap)].reshape(tokens, hdim)
        values = arrived[to, :, pl.ds((kv + k) * cap, cap)].reshape(tokens, hdim)
        return keys, values

    for j in range(1, lines):
        to = line_at(j)
        for i in order:
            mate = place_at(i)
            ship_in(to, mate).wait_recv()
        send(query, asked.at[to], ask_send.at[to], ask_recv.at[to], peer(to, place)).wait_recv()
        send(
            count.at[to], asked_count.at[to], count_send.at[to], count_recv.at[to], peer(to, place)
        ).wait_recv()
        set_bias = bias_of(asked_count[to].astype(jnp.float32) * filled(to))

        def set_head(k, carry):
            q = asked[to, :, :, pl.ds(k * group, group), :].reshape(rows, hdim)
            keys, values = arrivals(to, k)
            part, best, amount = partial(q, keys, values, set_bias)
            answer[to, k] = (part / amount).astype(jnp.bfloat16)
            log = best + jnp.log2(amount)
            answer_log[to, k] = jnp.sum(jnp.where(eye, log, 0.0), axis=0, keepdims=True)
            return carry

        lax.fori_loop(0, kv, set_head, 0)
        for copy in reply(j):
            copy.start()
        launch(j + 1, order[1:])
        if j + 2 <= lines:
            launch(j + 2, order[:1])

    def merge_head(k, carry):
        logs = []
        high = top[k]
        for j in range(1, lines):
            log = jnp.sum(jnp.where(eye, given_log[line_at(j), k], 0.0), axis=1, keepdims=True)
            logs.append(log)
            high = jnp.maximum(high, log)
        old = jnp.exp2(top[k] - high)
        whole = mixed[k] * old
        amount = total[k] * old
        for j in range(1, lines):
            share = jnp.exp2(logs[j - 1] - high)
            whole = whole + given[line_at(j), k].astype(jnp.float32) * share
            amount = amount + share
        mixed[k], total[k], top[k] = whole, amount, high
        return carry

    square[0] = jnp.zeros_like(square[0])

    def last_source(i):
        mate = place_at(i)
        if i > 0:
            ship_in(line, mate).wait_recv()
        here = arrived[line, mate, parts * kv * cap, 0:1, :].astype(jnp.float32)
        for m in range(plane):
            part = count[line, :, m * width : (m + 1) * width].astype(jnp.float32)
            mine_count = part if m == 0 else jnp.where(mate == m, part, mine_count)
        last_bias[...] = bias_of(mine_count * here[:, :width])

        def last_head(k, carry, mate=mate, last=i == (order[-1] if order else 0)):
            q = query[:, :, pl.ds(k * group, group), :].reshape(rows, hdim)
            keys = arrived[line, mate, pl.ds(k * cap, cap)].reshape(width, hdim)
            values = arrived[line, mate, pl.ds((kv + k) * cap, cap)].reshape(width, hdim)
            part, best, amount = partial(q, keys, values, last_bias[...])
            high = jnp.maximum(best, top[k])
            fresh, old = jnp.exp2(best - high), jnp.exp2(top[k] - high)
            whole = part * fresh + mixed[k] * old
            amount = amount * fresh + total[k] * old
            if not last:
                mixed[k], total[k], top[k] = whole, amount, high
                return carry
            result = (whole / amount).astype(jnp.bfloat16)
            attn[:, :, pl.ds(k * group, group), :] = result.reshape(steps, requests, group, hdim)
            wide = result.astype(jnp.float32)
            square[0] += jnp.sum((wide * wide).reshape(groups, group, hdim), axis=1)
            return carry

        lax.fori_loop(0, kv, last_head, 0)

    for i in [0] + order[:1]:
        last_source(i)
    for j in range(1, lines):
        to = line_at(j)
        send(answer.at[to], given.at[to], answer_send.at[to], answer_recv.at[to], peer(to, place)).wait_recv()
        send(answer_log.at[to], given_log.at[to], log_send.at[to], log_recv.at[to], peer(to, place)).wait_recv()
    lax.fori_loop(0, kv, merge_head, 0)
    for i in order[1:]:
        last_source(i)

    swap = send(square.at[0], square.at[1], square_sem.at[0], square_sem.at[1], {"tp": 1 - core})
    swap.start()
    swap.wait()
    mean = jnp.sum(square[0] + square[1], axis=-1, keepdims=True) / total_width
    scale = lax.rsqrt(mean + 1e-05)
    for t in range(steps):
        for g in range(requests):
            row = t * requests + g
            wide = attn[t, g].astype(jnp.float32)
            out[t, g] = (wide * scale[row : row + 1, :] * gain[...]).astype(out.dtype)

    for j in range(1, lines + 1):
        for i in range(1, plane):
            ship(j, i).wait_send()
        if j < lines:
            for copy in (ask(j), ask_counts(j)) + reply(j):
                copy.wait_send()


def attend(source, length, history, fill, switch, query, table, gain, tiles, tails, cap, plane, lines):
    steps, requests, heads, hdim = query.shape
    pool, parts, kv, page, _ = tiles.shape
    rows = steps * requests * heads // kv
    width = cap * page
    smem = pl.BlockSpec(memory_space=pltpu.SMEM)
    vmem = pl.BlockSpec(memory_space=pltpu.VMEM)
    dma = pltpu.SemaphoreType.DMA
    block = (parts * kv * cap + 1, page, hdim)
    return pl.pallas_call(
        functools.partial(attend_kernel, cap, plane, lines, heads * hdim * lax.axis_size("tp")),
        out_shape=jax.ShapeDtypeStruct(query.shape, jnp.bfloat16),
        in_specs=[smem] * 5 + [vmem] * 5,
        out_specs=vmem,
        scratch_shapes=[
            pltpu.VMEM((lines * plane,) + block, jnp.bfloat16),
            pltpu.VMEM((lines, steps * requests, plane * width), jnp.bfloat16),
            pltpu.VMEM((steps * requests, (pool + requests) * page), jnp.float32),
            pltpu.VMEM((steps * requests, width), jnp.float32),
            pltpu.VMEM((lines, plane) + block, jnp.bfloat16),
            pltpu.VMEM((lines,) + query.shape, jnp.bfloat16),
            pltpu.VMEM((lines, steps * requests, plane * width), jnp.bfloat16),
            pltpu.VMEM((lines, kv, rows, hdim), jnp.bfloat16),
            pltpu.VMEM((lines, kv, 1, rows), jnp.float32),
            pltpu.VMEM((lines, kv, rows, hdim), jnp.bfloat16),
            pltpu.VMEM((lines, kv, 1, rows), jnp.float32),
            pltpu.VMEM((kv, rows, hdim), jnp.float32),
            pltpu.VMEM((kv, rows, 1), jnp.float32),
            pltpu.VMEM((kv, rows, 1), jnp.float32),
            pltpu.VMEM(query.shape, jnp.bfloat16),
            pltpu.VMEM((2, steps * requests, hdim), jnp.float32),
            dma((lines, plane)),
            dma((lines, plane)),
        ]
        + [dma((lines,))] * 8
        + [dma((2,))],
        compiler_params=pltpu.CompilerParams(
            vmem_limit_bytes=VMEM_LIMIT, collective_id=0, has_side_effects=True
        ),
        name="attend",
    )(source, length, history, fill, switch, query, table, gain, tiles, tails)


def body(query, fresh, unfinished, store, table, history, fill, sender, target, switch, gain):
    replicas = lax.axis_size("rep")
    steps, requests, heads, hdim = query.shape
    cap = max(2, 2 * sender.shape[0] // replicas)
    plane = math.gcd(4, replicas)
    tiles = jnp.transpose(store, (0, 1, 3, 2, 4))
    source, length, tails = plan(
        sender, target.reshape(-1), fill, switch, jnp.transpose(unfinished, (0, 1, 3, 2, 4)), fresh,
        tiles, replicas, cap,
    )
    normed = attend(
        source, length, history, fill, switch, query, table, gain.reshape(heads, hdim), tiles, tails,
        cap, plane, replicas // plane,
    )
    return normed.reshape(steps, requests, heads * hdim)


def solution(mesh):
    placed = (
        P(None, "rep", "tp", None),
        P(None, "rep", None, "tp", None),
        P("rep", None, None, "tp", None),
        P("rep", None, None, "tp", None),
        P("rep", None),
        P("rep"),
        P("rep"),
        P("rep"),
        P("rep", None),
        P("rep"),
        P("tp"),
    )
    return jax.shard_map(
        body, mesh=mesh, in_specs=placed, out_specs=P(None, "rep", "tp"), check_vma=False
    )
```

```python
import functools
import math

import jax
import jax.numpy as jnp
from jax import lax
from jax.experimental import pallas as pl
from jax.experimental.pallas import tpu as pltpu
from jax.sharding import PartitionSpec as P

NEG = -1e30
LOG2E = 1.4426950408889634
VMEM_LIMIT = 50 * 1024 * 1024


def counts_of(table, history, first, pages, page):
    requests, entries = table.shape
    offset = lax.broadcasted_iota(jnp.int32, (page, entries), 0)
    position = lax.broadcasted_iota(jnp.int32, (page, entries), 1) * page + offset
    named = lax.broadcasted_iota(jnp.int32, (pages, entries), 0) + first
    per_page = []
    for g in range(requests):
        inside = jnp.where(position < history[g], 1.0, 0.0).astype(jnp.bfloat16)
        hit = jnp.where(table[g : g + 1, :] == named, 1.0, 0.0).astype(jnp.bfloat16)
        per_page.append(
            lax.dot_general(inside, hit, (((1,), (1,)), ((), ())), preferred_element_type=jnp.float32)
        )
    tokens = pages * page
    spread = (
        lax.broadcasted_iota(jnp.int32, (pages, tokens), 1) // page
        == lax.broadcasted_iota(jnp.int32, (pages, tokens), 0)
    )
    wide = jnp.dot(
        jnp.concatenate(per_page, 0).astype(jnp.bfloat16),
        jnp.where(spread, 1.0, 0.0).astype(jnp.bfloat16),
        preferred_element_type=jnp.float32,
    )
    own = (
        lax.broadcasted_iota(jnp.int32, (page, tokens), 1) % page
        == lax.broadcasted_iota(jnp.int32, (page, tokens), 0)
    )
    return [
        jnp.sum(jnp.where(own, wide[g * page : (g + 1) * page], 0.0), axis=0, keepdims=True)
        for g in range(requests)
    ]


def bias_of(count):
    return jnp.where(count > 0.0, jnp.log2(jnp.maximum(count, 1.0)), NEG)


def head_scores(query, keys, bias):
    rows, hdim = query.shape
    scores = lax.dot_general(query, keys, (((1,), (1,)), ((), ())), preferred_element_type=jnp.float32)
    groups = bias.shape[0]
    scores = scores.reshape(groups, rows // groups, -1) * (LOG2E / math.sqrt(hdim)) + bias[:, None, :]
    return scores.reshape(rows, -1)


def pack_kernel(
    cap, plane, sender, target, history, fill, switch, tiles, table, unfinished, fresh,
    out, count, bias, tails, held,
):
    replicas = out.shape[0]
    requests = fill.shape[0]
    pool, parts, kv, page, hdim = tiles.shape
    steps = bias.shape[0] // requests
    for d in range(replicas):
        held[d] = 0
    lane = lax.broadcasted_iota(jnp.int32, (page, hdim), 1)
    offset = lax.broadcasted_iota(jnp.int32, (page, hdim), 0)
    for g in range(requests):
        for c in range(parts):
            news = [fresh[s, g, c].astype(jnp.float32) for s in range(steps)]
            for k in range(kv):
                block = unfinished[g, c, k].astype(jnp.float32)
                for s in range(steps):
                    block = jnp.where(offset == fill[g] + s, news[s][k : k + 1, :], block)
                tails[g, c, k] = block.astype(tails.dtype)
    empty = jnp.zeros((page, hdim), out.dtype)
    for d in range(replicas):
        out[d, parts * kv * cap] = empty

    def place(e, carry):
        d = target[e]
        rank = held[d]
        held[d] = rank + 1
        source = sender[e]
        owner = jnp.maximum(source - pool, 0)
        for c in range(parts):
            for k in range(kv):
                out[d, (c * kv + k) * cap + rank] = jnp.where(
                    source >= pool, tails[owner, c, k], tiles[jnp.minimum(source, pool - 1), c, k]
                )
        length = jnp.where(source >= pool, fill[owner] + switch[owner], page)
        inside = (lane >= rank * page) & (lane < rank * page + length)
        mask = out[d, parts * kv * cap]
        out[d, parts * kv * cap] = jnp.where(inside, 1.0, mask.astype(jnp.float32)).astype(mask.dtype)
        return carry

    def clear(d, carry):
        def one(rank, carry):
            for block in range(parts * kv):
                out[d, block * cap + rank] = empty
            return carry

        return lax.fori_loop(held[d], cap, one, carry)

    lax.fori_loop(0, sender.shape[0], place, 0)
    lax.fori_loop(0, replicas, clear, 0)
    own = counts_of(table, history, 0, pool, page)
    tail = lax.broadcasted_iota(jnp.int32, (1, requests * page), 1)
    arrivals = counts_of(table, history, pool, replicas * cap, page)
    width = plane * cap * page
    for t in range(steps):
        for g in range(requests):
            row = t * requests + g
            bias[row : row + 1, : pool * page] = bias_of(own[g])
            seen = (tail // page == g) & (tail % page < fill[g] + t + 1)
            bias[row : row + 1, pool * page :] = jnp.where(seen, 0.0, NEG)
    for line in range(replicas // plane):
        rows = []
        for t in range(steps):
            for g in range(requests):
                part = arrivals[g][:, line * width : (line + 1) * width]
                rows.append(jnp.where(t >= switch[g], part, 0.0))
        count[line] = jnp.concatenate(rows, 0).astype(count.dtype)


def pack(tiles, sender, target, table, history, fill, switch, unfinished, fresh, replicas, cap, plane):
    pool, parts, kv, page, hdim = tiles.shape
    steps, requests = fresh.shape[:2]
    smem = pl.BlockSpec(memory_space=pltpu.SMEM)
    vmem = pl.BlockSpec(memory_space=pltpu.VMEM)
    return pl.pallas_call(
        functools.partial(pack_kernel, cap, plane),
        out_shape=(
            jax.ShapeDtypeStruct((replicas, parts * kv * cap + 1, page, hdim), tiles.dtype),
            jax.ShapeDtypeStruct((replicas // plane, steps * requests, plane * cap * page), jnp.bfloat16),
            jax.ShapeDtypeStruct((steps * requests, (pool + requests) * page), jnp.float32),
            jax.ShapeDtypeStruct(unfinished.shape, unfinished.dtype),
        ),
        in_specs=[smem] * 5 + [vmem] * 4,
        out_specs=(vmem, vmem, vmem, vmem),
        scratch_shapes=[pltpu.SMEM((replicas,), jnp.int32)],
        compiler_params=pltpu.CompilerParams(vmem_limit_bytes=VMEM_LIMIT),
        name="pack",
    )(sender, target, history, fill, switch, tiles, table, unfinished, fresh)


def partial(query, keys, values, bias):
    scores = head_scores(query, keys, bias)
    best = jnp.max(scores, axis=-1, keepdims=True)
    probs = jnp.exp2(scores - best)
    total = jnp.sum(probs, axis=-1, keepdims=True)
    return jnp.dot(probs.astype(jnp.bfloat16), values, preferred_element_type=jnp.float32), best, total


def diagonal(size):
    return lax.broadcasted_iota(jnp.int32, (size, size), 0) == lax.broadcasted_iota(jnp.int32, (size, size), 1)


def attend_kernel(
    cap, plane, lines, total_width,
    query, count, bias, gain, tiles, tails, outgoing,
    out,
    arrived, asked, asked_count, answer, answer_log, given, given_log, mixed, top, total, attn, square,
    own_sem, tile_send, tile_recv, ask_send, ask_recv, count_send, count_recv,
    answer_send, answer_recv, log_send, log_recv, square_sem,
):
    steps, requests, heads, hdim = query.shape
    pool, _, kv, page, _ = tiles.shape
    group = heads // kv
    groups = steps * requests
    rows = groups * group
    tokens = plane * cap * page
    me = lax.axis_index("rep")
    core = lax.axis_index("tp")
    line, place = lax.div(me, plane), lax.rem(me, plane)

    def peer(a_line, a_place):
        return {"rep": a_line * plane + a_place}

    def send(source, target, send_sem, recv_sem, device):
        return pltpu.make_async_remote_copy(
            src_ref=source, dst_ref=target, send_sem=send_sem, recv_sem=recv_sem,
            device_id=device, device_id_type=pl.DeviceIdType.MESH,
        )

    def line_at(step):
        return lax.rem(line + step, lines)

    def line_back(step):
        return lax.rem(line + lines - step, lines)

    def place_at(step):
        return lax.rem(place + step, plane)

    barrier = pltpu.get_barrier_semaphore()
    for j in range(1, lines):
        pl.semaphore_signal(barrier, inc=1, device_id=peer(line_at(j), place), device_id_type=pl.DeviceIdType.MESH)
    for i in range(1, plane):
        pl.semaphore_signal(barrier, inc=1, device_id=peer(line, place_at(i)), device_id_type=pl.DeviceIdType.MESH)
    pl.semaphore_signal(barrier, inc=1, device_id={"tp": 1 - core}, device_id_type=pl.DeviceIdType.MESH)
    pl.semaphore_wait(barrier, lines + plane - 1)

    def ask(j):
        to = line_at(j)
        return (
            send(query, asked.at[line], ask_send.at[to], ask_recv.at[line], peer(to, place)),
            send(count.at[to], asked_count.at[line], count_send.at[to], count_recv.at[line], peer(to, place)),
        )

    def ship(j, i):
        to = line_at(j)
        mate = place_at(i)
        return send(
            outgoing.at[to * plane + mate], arrived.at[to, place],
            tile_send.at[to, mate], tile_recv.at[to, place], peer(line, mate),
        )

    def keep(j):
        to = line_at(j)
        return pltpu.make_async_copy(outgoing.at[to * plane + place], arrived.at[to, place], own_sem.at[to])

    def reply(j):
        to = line_at(j)
        return (
            send(answer.at[to], given.at[line], answer_send.at[to], answer_recv.at[line], peer(to, place)),
            send(answer_log.at[to], given_log.at[line], log_send.at[to], log_recv.at[line], peer(to, place)),
        )

    for j in range(1, lines + 1):
        for i in range(1, plane):
            ship(j, i).start()
        keep(j).start()
        if j < lines:
            for copy in ask(lines - j):
                copy.start()

    def pool_head(k, carry):
        q = query[:, :, pl.ds(k * group, group), :].reshape(rows, hdim)
        both = [
            jnp.concatenate(
                [tiles[:, c, k].reshape(pool * page, hdim), tails[:, c, k].reshape(requests * page, hdim)], 0
            )
            for c in range(2)
        ]
        mixed[k], top[k], total[k] = partial(q, both[0], both[1], bias[...])
        return carry

    lax.fori_loop(0, kv, pool_head, 0)

    width = cap * page
    repeat = (
        lax.broadcasted_iota(jnp.int32, (hdim, tokens), 1) % width
        == lax.broadcasted_iota(jnp.int32, (hdim, tokens), 0)
    )
    repeat = jnp.where(repeat, 1.0, 0.0).astype(jnp.bfloat16)
    mine = (
        lax.broadcasted_iota(jnp.int32, (plane, tokens), 1) // width
        == lax.broadcasted_iota(jnp.int32, (plane, tokens), 0)
    )
    eye = diagonal(rows)

    def filled(to):
        here = arrived[to, :, 2 * kv * cap, 0, :]
        spread = jnp.dot(here, repeat, preferred_element_type=jnp.float32)
        return jnp.sum(jnp.where(mine, spread, 0.0), axis=0, keepdims=True)

    def arrivals(to, k):
        keys = arrived[to, :, pl.ds(k * cap, cap)].reshape(tokens, hdim)
        values = arrived[to, :, pl.ds((kv + k) * cap, cap)].reshape(tokens, hdim)
        return keys, values

    for j in range(1, lines):
        to = line_at(j)
        for i in range(1, plane):
            source = place_at(i)
            send(
                outgoing.at[0], arrived.at[to, source], tile_send.at[to, source], tile_recv.at[to, source],
                peer(line, source),
            ).wait_recv()
        keep(j).wait()
        send(query, asked.at[to], ask_send.at[to], ask_recv.at[to], peer(to, place)).wait_recv()
        send(
            count.at[to], asked_count.at[to], count_send.at[to], count_recv.at[to], peer(to, place)
        ).wait_recv()
        set_bias = bias_of(asked_count[to].astype(jnp.float32) * filled(to))

        def set_head(k, carry):
            q = asked[to, :, :, pl.ds(k * group, group), :].reshape(rows, hdim)
            keys, values = arrivals(to, k)
            part, best, amount = partial(q, keys, values, set_bias)
            answer[to, k] = (part / amount).astype(jnp.bfloat16)
            log = best + jnp.log2(amount)
            answer_log[to, k] = jnp.sum(jnp.where(eye, log, 0.0), axis=0, keepdims=True)
            return carry

        lax.fori_loop(0, kv, set_head, 0)
        for copy in reply(j):
            copy.start()

    for i in range(1, plane):
        source = place_at(i)
        send(
            outgoing.at[0], arrived.at[line, source], tile_send.at[line, source], tile_recv.at[line, source],
            peer(line, source),
        ).wait_recv()
    keep(lines).wait()
    last_bias = bias_of(count[line].astype(jnp.float32) * filled(line))

    def last_head(k, carry):
        q = query[:, :, pl.ds(k * group, group), :].reshape(rows, hdim)
        keys, values = arrivals(line, k)
        part, best, amount = partial(q, keys, values, last_bias)
        high = jnp.maximum(best, top[k])
        fresh, old = jnp.exp2(best - high), jnp.exp2(top[k] - high)
        mixed[k] = part * fresh + mixed[k] * old
        total[k] = amount * fresh + total[k] * old
        top[k] = high
        return carry

    lax.fori_loop(0, kv, last_head, 0)

    for j in range(1, lines):
        to = line_at(j)
        send(answer.at[to], given.at[to], answer_send.at[to], answer_recv.at[to], peer(to, place)).wait_recv()
        send(answer_log.at[to], given_log.at[to], log_send.at[to], log_recv.at[to], peer(to, place)).wait_recv()

    square[0] = jnp.zeros_like(square[0])

    def merge_head(k, carry):
        logs = []
        high = top[k]
        for j in range(1, lines):
            log = jnp.sum(jnp.where(eye, given_log[line_at(j), k], 0.0), axis=1, keepdims=True)
            logs.append(log)
            high = jnp.maximum(high, log)
        old = jnp.exp2(top[k] - high)
        whole = mixed[k] * old
        amount = total[k] * old
        for j in range(1, lines):
            share = jnp.exp2(logs[j - 1] - high)
            whole = whole + given[line_at(j), k].astype(jnp.float32) * share
            amount = amount + share
        result = (whole / amount).astype(jnp.bfloat16)
        attn[:, :, pl.ds(k * group, group), :] = result.reshape(steps, requests, group, hdim)
        wide = result.astype(jnp.float32)
        square[0] += jnp.sum((wide * wide).reshape(groups, group, hdim), axis=1)
        return carry

    lax.fori_loop(0, kv, merge_head, 0)
    swap = send(square.at[0], square.at[1], square_sem.at[0], square_sem.at[1], {"tp": 1 - core})
    swap.start()
    swap.wait()
    mean = jnp.sum(square[0] + square[1], axis=-1, keepdims=True) / total_width
    scale = lax.rsqrt(mean + 1e-05)
    for t in range(steps):
        for g in range(requests):
            row = t * requests + g
            wide = attn[t, g].astype(jnp.float32)
            out[t, g] = (wide * scale[row : row + 1, :] * gain[...]).astype(out.dtype)

    for j in range(1, lines + 1):
        for i in range(1, plane):
            ship(j, i).wait_send()
        if j < lines:
            for copy in ask(j) + reply(j):
                copy.wait_send()


def attend(query, count, bias, gain, tiles, tails, outgoing, cap, plane):
    steps, requests, heads, hdim = query.shape
    kv, page = tiles.shape[2:4]
    lines = outgoing.shape[0] // plane
    rows = steps * requests * heads // kv
    vmem = pl.BlockSpec(memory_space=pltpu.VMEM)
    dma = pltpu.SemaphoreType.DMA
    return pl.pallas_call(
        functools.partial(attend_kernel, cap, plane, lines, heads * hdim * lax.axis_size("tp")),
        out_shape=jax.ShapeDtypeStruct(query.shape, jnp.bfloat16),
        in_specs=[vmem] * 6 + [pl.BlockSpec(memory_space=pl.ANY)],
        out_specs=vmem,
        scratch_shapes=[
            pltpu.VMEM((lines, plane) + outgoing.shape[1:], jnp.bfloat16),
            pltpu.VMEM((lines,) + query.shape, jnp.bfloat16),
            pltpu.VMEM(count.shape, jnp.bfloat16),
            pltpu.VMEM((lines, kv, rows, hdim), jnp.bfloat16),
            pltpu.VMEM((lines, kv, 1, rows), jnp.float32),
            pltpu.VMEM((lines, kv, rows, hdim), jnp.bfloat16),
            pltpu.VMEM((lines, kv, 1, rows), jnp.float32),
            pltpu.VMEM((kv, rows, hdim), jnp.float32),
            pltpu.VMEM((kv, rows, 1), jnp.float32),
            pltpu.VMEM((kv, rows, 1), jnp.float32),
            pltpu.VMEM(query.shape, jnp.bfloat16),
            pltpu.VMEM((2, steps * requests, hdim), jnp.float32),
            dma((lines,)),
            dma((lines, plane)),
            dma((lines, plane)),
        ]
        + [dma((lines,))] * 8
        + [dma((2,))],
        compiler_params=pltpu.CompilerParams(
            vmem_limit_bytes=VMEM_LIMIT, collective_id=0, has_side_effects=True
        ),
        name="attend",
    )(query, count, bias, gain, tiles, tails, outgoing)


def body(query, fresh, unfinished, store, table, history, fill, sender, target, switch, gain):
    replicas = lax.axis_size("rep")
    steps, requests, heads, hdim = query.shape
    cap = max(2, 2 * sender.shape[0] // replicas)
    plane = math.gcd(4, replicas)
    tiles = jnp.transpose(store, (0, 1, 3, 2, 4))
    outgoing, count, bias, tails = pack(
        tiles, sender, target.reshape(-1), table, history, fill, switch,
        jnp.transpose(unfinished, (0, 1, 3, 2, 4)), fresh, replicas, cap, plane,
    )
    normed = attend(query, count, bias, gain.reshape(heads, hdim), tiles, tails, outgoing, cap, plane)
    return normed.reshape(steps, requests, heads * hdim)


def solution(mesh):
    placed = (
        P(None, "rep", "tp", None),
        P(None, "rep", None, "tp", None),
        P("rep", None, None, "tp", None),
        P("rep", None, None, "tp", None),
        P("rep", None),
        P("rep"),
        P("rep"),
        P("rep"),
        P("rep", None),
        P("rep"),
        P("tp"),
    )
    return jax.shard_map(
        body, mesh=mesh, in_specs=placed, out_specs=P(None, "rep", "tp"), check_vma=False
    )
```

```python
import functools
import math

import jax
import jax.numpy as jnp
from jax import lax
from jax.experimental import pallas as pl
from jax.experimental.pallas import tpu as pltpu
from jax.sharding import PartitionSpec as P

NEG = -1e30
LOG2E = 1.4426950408889634
VMEM_LIMIT = 50 * 1024 * 1024


def counts_of(table, history, first, pages, page):
    requests, entries = table.shape
    offset = lax.broadcasted_iota(jnp.int32, (page, entries), 0)
    position = lax.broadcasted_iota(jnp.int32, (page, entries), 1) * page + offset
    named = lax.broadcasted_iota(jnp.int32, (pages, entries), 0) + first
    per_page = []
    for g in range(requests):
        inside = jnp.where(position < history[g], 1.0, 0.0).astype(jnp.bfloat16)
        hit = jnp.where(table[g : g + 1, :] == named, 1.0, 0.0).astype(jnp.bfloat16)
        per_page.append(
            lax.dot_general(inside, hit, (((1,), (1,)), ((), ())), preferred_element_type=jnp.float32)
        )
    tokens = pages * page
    spread = (
        lax.broadcasted_iota(jnp.int32, (pages, tokens), 1) // page
        == lax.broadcasted_iota(jnp.int32, (pages, tokens), 0)
    )
    wide = jnp.dot(
        jnp.concatenate(per_page, 0).astype(jnp.bfloat16),
        jnp.where(spread, 1.0, 0.0).astype(jnp.bfloat16),
        preferred_element_type=jnp.float32,
    )
    own = (
        lax.broadcasted_iota(jnp.int32, (page, tokens), 1) % page
        == lax.broadcasted_iota(jnp.int32, (page, tokens), 0)
    )
    return [
        jnp.sum(jnp.where(own, wide[g * page : (g + 1) * page], 0.0), axis=0, keepdims=True)
        for g in range(requests)
    ]


def bias_of(count):
    return jnp.where(count > 0.0, jnp.log2(jnp.maximum(count, 1.0)), NEG)


def head_scores(query, keys, bias):
    rows, hdim = query.shape
    scores = lax.dot_general(query, keys, (((1,), (1,)), ((), ())), preferred_element_type=jnp.float32)
    groups = bias.shape[0]
    scores = scores.reshape(groups, rows // groups, -1) * (LOG2E / math.sqrt(hdim)) + bias[:, None, :]
    return scores.reshape(rows, -1)


def pack_kernel(
    cap, sender, target, fill, switch, tiles, unfinished, fresh, out, tails, held,
):
    replicas = out.shape[0]
    requests = fill.shape[0]
    pool, parts, kv, page, hdim = tiles.shape
    steps = fresh.shape[0]
    for d in range(replicas):
        held[d] = 0
    lane = lax.broadcasted_iota(jnp.int32, (page, hdim), 1)
    offset = lax.broadcasted_iota(jnp.int32, (page, hdim), 0)
    for g in range(requests):
        for c in range(parts):
            news = [fresh[s, g, c].astype(jnp.float32) for s in range(steps)]
            for k in range(kv):
                block = unfinished[g, c, k].astype(jnp.float32)
                for s in range(steps):
                    block = jnp.where(offset == fill[g] + s, news[s][k : k + 1, :], block)
                tails[g, c, k] = block.astype(tails.dtype)
    empty = jnp.zeros((page, hdim), out.dtype)
    for d in range(replicas):
        out[d, parts * kv * cap] = empty

    def place(e, carry):
        d = target[e]
        rank = held[d]
        held[d] = rank + 1
        source = sender[e]
        owner = jnp.maximum(source - pool, 0)
        for c in range(parts):
            for k in range(kv):
                out[d, (c * kv + k) * cap + rank] = jnp.where(
                    source >= pool, tails[owner, c, k], tiles[jnp.minimum(source, pool - 1), c, k]
                )
        length = jnp.where(source >= pool, fill[owner] + switch[owner], page)
        inside = (lane >= rank * page) & (lane < rank * page + length)
        mask = out[d, parts * kv * cap]
        out[d, parts * kv * cap] = jnp.where(inside, 1.0, mask.astype(jnp.float32)).astype(mask.dtype)
        return carry

    def clear(d, carry):
        def one(rank, carry):
            for block in range(parts * kv):
                out[d, block * cap + rank] = empty
            return carry

        return lax.fori_loop(held[d], cap, one, carry)

    lax.fori_loop(0, sender.shape[0], place, 0)
    lax.fori_loop(0, replicas, clear, 0)


def pack(tiles, sender, target, fill, switch, unfinished, fresh, replicas, cap):
    pool, parts, kv, page, hdim = tiles.shape
    smem = pl.BlockSpec(memory_space=pltpu.SMEM)
    vmem = pl.BlockSpec(memory_space=pltpu.VMEM)
    return pl.pallas_call(
        functools.partial(pack_kernel, cap),
        out_shape=(
            jax.ShapeDtypeStruct((replicas, parts * kv * cap + 1, page, hdim), tiles.dtype),
            jax.ShapeDtypeStruct(unfinished.shape, unfinished.dtype),
        ),
        in_specs=[smem] * 4 + [vmem] * 3,
        out_specs=(vmem, vmem),
        scratch_shapes=[pltpu.SMEM((replicas,), jnp.int32)],
        compiler_params=pltpu.CompilerParams(vmem_limit_bytes=VMEM_LIMIT),
        name="pack",
    )(sender, target, fill, switch, tiles, unfinished, fresh)


def partial(query, keys, values, bias):
    scores = head_scores(query, keys, bias)
    best = jnp.max(scores, axis=-1, keepdims=True)
    probs = jnp.exp2(scores - best)
    total = jnp.sum(probs, axis=-1, keepdims=True)
    return jnp.dot(probs.astype(jnp.bfloat16), values, preferred_element_type=jnp.float32), best, total


def diagonal(size):
    return lax.broadcasted_iota(jnp.int32, (size, size), 0) == lax.broadcasted_iota(jnp.int32, (size, size), 1)


def attend_kernel(
    cap, plane, lines, total_width,
    history, fill, switch,
    query, table, gain, tiles, tails, outgoing,
    out,
    count, bias, arrived, asked, asked_count, answer, answer_log, given, given_log, mixed, top, total, attn, square,
    own_sem, tile_send, tile_recv, ask_send, ask_recv, count_send, count_recv,
    answer_send, answer_recv, log_send, log_recv, square_sem,
):
    steps, requests, heads, hdim = query.shape
    pool, _, kv, page, _ = tiles.shape
    group = heads // kv
    groups = steps * requests
    rows = groups * group
    tokens = plane * cap * page
    me = lax.axis_index("rep")
    core = lax.axis_index("tp")
    line, place = lax.div(me, plane), lax.rem(me, plane)

    def peer(a_line, a_place):
        return {"rep": a_line * plane + a_place}

    def send(source, target, send_sem, recv_sem, device):
        return pltpu.make_async_remote_copy(
            src_ref=source, dst_ref=target, send_sem=send_sem, recv_sem=recv_sem,
            device_id=device, device_id_type=pl.DeviceIdType.MESH,
        )

    def line_at(step):
        return lax.rem(line + step, lines)

    def line_back(step):
        return lax.rem(line + lines - step, lines)

    def place_at(step):
        return lax.rem(place + step, plane)

    barrier = pltpu.get_barrier_semaphore()
    for j in range(1, lines):
        pl.semaphore_signal(barrier, inc=1, device_id=peer(line_at(j), place), device_id_type=pl.DeviceIdType.MESH)
    for i in range(1, plane):
        pl.semaphore_signal(barrier, inc=1, device_id=peer(line, place_at(i)), device_id_type=pl.DeviceIdType.MESH)
    pl.semaphore_signal(barrier, inc=1, device_id={"tp": 1 - core}, device_id_type=pl.DeviceIdType.MESH)
    pl.semaphore_wait(barrier, lines + plane - 1)

    def ask(j):
        to = line_at(j)
        return send(query, asked.at[line], ask_send.at[to], ask_recv.at[line], peer(to, place))

    def ask_counts(j):
        to = line_at(j)
        return send(
            count.at[to], asked_count.at[line], count_send.at[to], count_recv.at[line], peer(to, place)
        )

    def ship(j, i):
        to = line_at(j)
        mate = place_at(i)
        return send(
            outgoing.at[to * plane + mate], arrived.at[to, place],
            tile_send.at[to, mate], tile_recv.at[to, place], peer(line, mate),
        )

    def keep(j):
        to = line_at(j)
        return pltpu.make_async_copy(outgoing.at[to * plane + place], arrived.at[to, place], own_sem.at[to])

    def reply(j):
        to = line_at(j)
        return (
            send(answer.at[to], given.at[line], answer_send.at[to], answer_recv.at[line], peer(to, place)),
            send(answer_log.at[to], given_log.at[line], log_send.at[to], log_recv.at[line], peer(to, place)),
        )

    def launch(j):
        for i in range(1, plane):
            ship(j, i).start()
        keep(j).start()

    if lines > 1:
        launch(1)
    for j in range(1, lines):
        ask(lines - j).start()

    tokens_in = counts_of(table, history, pool, lines * plane * cap, page)
    for to in range(lines):
        parts_of = [
            jnp.where(t >= switch[g], tokens_in[g][:, to * tokens : (to + 1) * tokens], 0.0)
            for t in range(steps)
            for g in range(requests)
        ]
        count[to] = jnp.concatenate(parts_of, 0).astype(count.dtype)
    for j in range(1, lines):
        ask_counts(lines - j).start()
    for j in range(2, lines):
        launch(j)
    keep(lines).start()
    for i in range(lines, plane):
        ship(lines, i).start()

    own = counts_of(table, history, 0, pool, page)
    tail = lax.broadcasted_iota(jnp.int32, (1, requests * page), 1)
    for t in range(steps):
        for g in range(requests):
            row = t * requests + g
            bias[row : row + 1, : pool * page] = bias_of(own[g])
            seen = (tail // page == g) & (tail % page < fill[g] + t + 1)
            bias[row : row + 1, pool * page :] = jnp.where(seen, 0.0, NEG)

    def pool_head(k, carry):
        q = query[:, :, pl.ds(k * group, group), :].reshape(rows, hdim)
        both = [
            jnp.concatenate(
                [tiles[:, c, k].reshape(pool * page, hdim), tails[:, c, k].reshape(requests * page, hdim)], 0
            )
            for c in range(2)
        ]
        mixed[k], top[k], total[k] = partial(q, both[0], both[1], bias[...])
        return carry

    lax.fori_loop(0, kv, pool_head, 0)

    width = cap * page
    repeat = (
        lax.broadcasted_iota(jnp.int32, (hdim, tokens), 1) % width
        == lax.broadcasted_iota(jnp.int32, (hdim, tokens), 0)
    )
    repeat = jnp.where(repeat, 1.0, 0.0).astype(jnp.bfloat16)
    mine = (
        lax.broadcasted_iota(jnp.int32, (plane, tokens), 1) // width
        == lax.broadcasted_iota(jnp.int32, (plane, tokens), 0)
    )
    eye = diagonal(rows)

    def filled(to):
        here = arrived[to, :, 2 * kv * cap, 0, :]
        spread = jnp.dot(here, repeat, preferred_element_type=jnp.float32)
        return jnp.sum(jnp.where(mine, spread, 0.0), axis=0, keepdims=True)

    def arrivals(to, k):
        keys = arrived[to, :, pl.ds(k * cap, cap)].reshape(tokens, hdim)
        values = arrived[to, :, pl.ds((kv + k) * cap, cap)].reshape(tokens, hdim)
        return keys, values

    for j in range(1, lines):
        to = line_at(j)
        for i in range(1, plane):
            source = place_at(i)
            send(
                outgoing.at[0], arrived.at[to, source], tile_send.at[to, source], tile_recv.at[to, source],
                peer(line, source),
            ).wait_recv()
        keep(j).wait()
        send(query, asked.at[to], ask_send.at[to], ask_recv.at[to], peer(to, place)).wait_recv()
        send(
            count.at[to], asked_count.at[to], count_send.at[to], count_recv.at[to], peer(to, place)
        ).wait_recv()
        set_bias = bias_of(asked_count[to].astype(jnp.float32) * filled(to))

        def set_head(k, carry):
            q = asked[to, :, :, pl.ds(k * group, group), :].reshape(rows, hdim)
            keys, values = arrivals(to, k)
            part, best, amount = partial(q, keys, values, set_bias)
            answer[to, k] = (part / amount).astype(jnp.bfloat16)
            log = best + jnp.log2(amount)
            answer_log[to, k] = jnp.sum(jnp.where(eye, log, 0.0), axis=0, keepdims=True)
            return carry

        lax.fori_loop(0, kv, set_head, 0)
        for copy in reply(j):
            copy.start()
        if j < plane:
            ship(lines, j).start()

    for j in range(1, lines):
        to = line_at(j)
        send(answer.at[to], given.at[to], answer_send.at[to], answer_recv.at[to], peer(to, place)).wait_recv()
        send(answer_log.at[to], given_log.at[to], log_send.at[to], log_recv.at[to], peer(to, place)).wait_recv()

    def merge_head(k, carry):
        logs = []
        high = top[k]
        for j in range(1, lines):
            log = jnp.sum(jnp.where(eye, given_log[line_at(j), k], 0.0), axis=1, keepdims=True)
            logs.append(log)
            high = jnp.maximum(high, log)
        old = jnp.exp2(top[k] - high)
        whole = mixed[k] * old
        amount = total[k] * old
        for j in range(1, lines):
            share = jnp.exp2(logs[j - 1] - high)
            whole = whole + given[line_at(j), k].astype(jnp.float32) * share
            amount = amount + share
        mixed[k], total[k], top[k] = whole, amount, high
        return carry

    lax.fori_loop(0, kv, merge_head, 0)
    square[0] = jnp.zeros_like(square[0])

    for i in range(1, plane):
        source = place_at(i)
        send(
            outgoing.at[0], arrived.at[line, source], tile_send.at[line, source], tile_recv.at[line, source],
            peer(line, source),
        ).wait_recv()
    keep(lines).wait()
    last_bias = bias_of(count[line].astype(jnp.float32) * filled(line))

    def last_head(k, carry):
        q = query[:, :, pl.ds(k * group, group), :].reshape(rows, hdim)
        keys, values = arrivals(line, k)
        part, best, amount = partial(q, keys, values, last_bias)
        high = jnp.maximum(best, top[k])
        fresh, old = jnp.exp2(best - high), jnp.exp2(top[k] - high)
        whole = part * fresh + mixed[k] * old
        result = (whole / (amount * fresh + total[k] * old)).astype(jnp.bfloat16)
        attn[:, :, pl.ds(k * group, group), :] = result.reshape(steps, requests, group, hdim)
        wide = result.astype(jnp.float32)
        square[0] += jnp.sum((wide * wide).reshape(groups, group, hdim), axis=1)
        return carry

    lax.fori_loop(0, kv, last_head, 0)
    swap = send(square.at[0], square.at[1], square_sem.at[0], square_sem.at[1], {"tp": 1 - core})
    swap.start()
    swap.wait()
    mean = jnp.sum(square[0] + square[1], axis=-1, keepdims=True) / total_width
    scale = lax.rsqrt(mean + 1e-05)
    for t in range(steps):
        for g in range(requests):
            row = t * requests + g
            wide = attn[t, g].astype(jnp.float32)
            out[t, g] = (wide * scale[row : row + 1, :] * gain[...]).astype(out.dtype)

    for j in range(1, lines + 1):
        for i in range(1, plane):
            ship(j, i).wait_send()
        if j < lines:
            for copy in (ask(j), ask_counts(j)) + reply(j):
                copy.wait_send()


def attend(history, fill, switch, query, table, gain, tiles, tails, outgoing, cap, plane):
    steps, requests, heads, hdim = query.shape
    kv, page = tiles.shape[2:4]
    lines = outgoing.shape[0] // plane
    rows = steps * requests * heads // kv
    counts = (lines, steps * requests, plane * cap * page)
    smem = pl.BlockSpec(memory_space=pltpu.SMEM)
    vmem = pl.BlockSpec(memory_space=pltpu.VMEM)
    dma = pltpu.SemaphoreType.DMA
    return pl.pallas_call(
        functools.partial(attend_kernel, cap, plane, lines, heads * hdim * lax.axis_size("tp")),
        out_shape=jax.ShapeDtypeStruct(query.shape, jnp.bfloat16),
        in_specs=[smem] * 3 + [vmem] * 5 + [pl.BlockSpec(memory_space=pl.ANY)],
        out_specs=vmem,
        scratch_shapes=[
            pltpu.VMEM(counts, jnp.bfloat16),
            pltpu.VMEM((steps * requests, (tiles.shape[0] + requests) * page), jnp.float32),
            pltpu.VMEM((lines, plane) + outgoing.shape[1:], jnp.bfloat16),
            pltpu.VMEM((lines,) + query.shape, jnp.bfloat16),
            pltpu.VMEM(counts, jnp.bfloat16),
            pltpu.VMEM((lines, kv, rows, hdim), jnp.bfloat16),
            pltpu.VMEM((lines, kv, 1, rows), jnp.float32),
            pltpu.VMEM((lines, kv, rows, hdim), jnp.bfloat16),
            pltpu.VMEM((lines, kv, 1, rows), jnp.float32),
            pltpu.VMEM((kv, rows, hdim), jnp.float32),
            pltpu.VMEM((kv, rows, 1), jnp.float32),
            pltpu.VMEM((kv, rows, 1), jnp.float32),
            pltpu.VMEM(query.shape, jnp.bfloat16),
            pltpu.VMEM((2, steps * requests, hdim), jnp.float32),
            dma((lines,)),
            dma((lines, plane)),
            dma((lines, plane)),
        ]
        + [dma((lines,))] * 8
        + [dma((2,))],
        compiler_params=pltpu.CompilerParams(
            vmem_limit_bytes=VMEM_LIMIT, collective_id=0, has_side_effects=True
        ),
        name="attend",
    )(history, fill, switch, query, table, gain, tiles, tails, outgoing)


def body(query, fresh, unfinished, store, table, history, fill, sender, target, switch, gain):
    replicas = lax.axis_size("rep")
    steps, requests, heads, hdim = query.shape
    cap = max(2, 2 * sender.shape[0] // replicas)
    plane = math.gcd(4, replicas)
    tiles = jnp.transpose(store, (0, 1, 3, 2, 4))
    outgoing, tails = pack(
        tiles, sender, target.reshape(-1), fill, switch,
        jnp.transpose(unfinished, (0, 1, 3, 2, 4)), fresh, replicas, cap,
    )
    normed = attend(
        history, fill, switch, query, table, gain.reshape(heads, hdim), tiles, tails, outgoing, cap, plane
    )
    return normed.reshape(steps, requests, heads * hdim)


def solution(mesh):
    placed = (
        P(None, "rep", "tp", None),
        P(None, "rep", None, "tp", None),
        P("rep", None, None, "tp", None),
        P("rep", None, None, "tp", None),
        P("rep", None),
        P("rep"),
        P("rep"),
        P("rep"),
        P("rep", None),
        P("rep"),
        P("tp"),
    )
    return jax.shard_map(
        body, mesh=mesh, in_specs=placed, out_specs=P(None, "rep", "tp"), check_vma=False
    )
```

```python
import functools
import math

import jax
import jax.numpy as jnp
from jax import lax
from jax.experimental import pallas as pl
from jax.experimental.pallas import tpu as pltpu
from jax.sharding import PartitionSpec as P

NEG = -1e30
LOG2E = 1.4426950408889634
VMEM_LIMIT = 50 * 1024 * 1024


def counts_of(table, history, first, pages, page):
    requests, entries = table.shape
    offset = lax.broadcasted_iota(jnp.int32, (page, entries), 0)
    position = lax.broadcasted_iota(jnp.int32, (page, entries), 1) * page + offset
    named = lax.broadcasted_iota(jnp.int32, (pages, entries), 0) + first
    per_page = []
    for g in range(requests):
        inside = jnp.where(position < history[g], 1.0, 0.0).astype(jnp.bfloat16)
        hit = jnp.where(table[g : g + 1, :] == named, 1.0, 0.0).astype(jnp.bfloat16)
        per_page.append(
            lax.dot_general(inside, hit, (((1,), (1,)), ((), ())), preferred_element_type=jnp.float32)
        )
    tokens = pages * page
    spread = (
        lax.broadcasted_iota(jnp.int32, (pages, tokens), 1) // page
        == lax.broadcasted_iota(jnp.int32, (pages, tokens), 0)
    )
    wide = jnp.dot(
        jnp.concatenate(per_page, 0).astype(jnp.bfloat16),
        jnp.where(spread, 1.0, 0.0).astype(jnp.bfloat16),
        preferred_element_type=jnp.float32,
    )
    own = (
        lax.broadcasted_iota(jnp.int32, (page, tokens), 1) % page
        == lax.broadcasted_iota(jnp.int32, (page, tokens), 0)
    )
    return [
        jnp.sum(jnp.where(own, wide[g * page : (g + 1) * page], 0.0), axis=0, keepdims=True)
        for g in range(requests)
    ]


def bias_of(count):
    return jnp.where(count > 0.0, jnp.log2(jnp.maximum(count, 1.0)), NEG)


def head_scores(query, keys, bias):
    rows, hdim = query.shape
    scores = lax.dot_general(query, keys, (((1,), (1,)), ((), ())), preferred_element_type=jnp.float32)
    groups = bias.shape[0]
    scores = scores.reshape(groups, rows // groups, -1) * (LOG2E / math.sqrt(hdim)) + bias[:, None, :]
    return scores.reshape(rows, -1)


def pack_kernel(
    cap, plane, sender, target, history, fill, switch, tiles, table, unfinished, fresh,
    out, count, bias, tails, held,
):
    replicas = out.shape[0]
    requests = fill.shape[0]
    pool, parts, kv, page, hdim = tiles.shape
    steps = bias.shape[0] // requests
    for d in range(replicas):
        held[d] = 0
    lane = lax.broadcasted_iota(jnp.int32, (page, hdim), 1)
    offset = lax.broadcasted_iota(jnp.int32, (page, hdim), 0)
    for g in range(requests):
        for c in range(parts):
            news = [fresh[s, g, c].astype(jnp.float32) for s in range(steps)]
            for k in range(kv):
                block = unfinished[g, c, k].astype(jnp.float32)
                for s in range(steps):
                    block = jnp.where(offset == fill[g] + s, news[s][k : k + 1, :], block)
                tails[g, c, k] = block.astype(tails.dtype)
    empty = jnp.zeros((page, hdim), out.dtype)
    for d in range(replicas):
        out[d, parts * kv * cap] = empty

    def place(e, carry):
        d = target[e]
        rank = held[d]
        held[d] = rank + 1
        source = sender[e]
        owner = jnp.maximum(source - pool, 0)
        for c in range(parts):
            for k in range(kv):
                out[d, (c * kv + k) * cap + rank] = jnp.where(
                    source >= pool, tails[owner, c, k], tiles[jnp.minimum(source, pool - 1), c, k]
                )
        length = jnp.where(source >= pool, fill[owner] + switch[owner], page)
        inside = (lane >= rank * page) & (lane < rank * page + length)
        mask = out[d, parts * kv * cap]
        out[d, parts * kv * cap] = jnp.where(inside, 1.0, mask.astype(jnp.float32)).astype(mask.dtype)
        return carry

    def clear(d, carry):
        def one(rank, carry):
            for block in range(parts * kv):
                out[d, block * cap + rank] = empty
            return carry

        return lax.fori_loop(held[d], cap, one, carry)

    lax.fori_loop(0, sender.shape[0], place, 0)
    lax.fori_loop(0, replicas, clear, 0)
    own = counts_of(table, history, 0, pool, page)
    tail = lax.broadcasted_iota(jnp.int32, (1, requests * page), 1)
    arrivals = counts_of(table, history, pool, replicas * cap, page)
    width = plane * cap * page
    for t in range(steps):
        for g in range(requests):
            row = t * requests + g
            bias[row : row + 1, : pool * page] = bias_of(own[g])
            seen = (tail // page == g) & (tail % page < fill[g] + t + 1)
            bias[row : row + 1, pool * page :] = jnp.where(seen, 0.0, NEG)
    for line in range(replicas // plane):
        rows = []
        for t in range(steps):
            for g in range(requests):
                part = arrivals[g][:, line * width : (line + 1) * width]
                rows.append(jnp.where(t >= switch[g], part, 0.0))
        count[line] = jnp.concatenate(rows, 0).astype(count.dtype)


def pack(tiles, sender, target, table, history, fill, switch, unfinished, fresh, replicas, cap, plane):
    pool, parts, kv, page, hdim = tiles.shape
    steps, requests = fresh.shape[:2]
    smem = pl.BlockSpec(memory_space=pltpu.SMEM)
    vmem = pl.BlockSpec(memory_space=pltpu.VMEM)
    return pl.pallas_call(
        functools.partial(pack_kernel, cap, plane),
        out_shape=(
            jax.ShapeDtypeStruct((replicas, parts * kv * cap + 1, page, hdim), tiles.dtype),
            jax.ShapeDtypeStruct((replicas // plane, steps * requests, plane * cap * page), jnp.bfloat16),
            jax.ShapeDtypeStruct((steps * requests, (pool + requests) * page), jnp.float32),
            jax.ShapeDtypeStruct(unfinished.shape, unfinished.dtype),
        ),
        in_specs=[smem] * 5 + [vmem] * 4,
        out_specs=(vmem, vmem, vmem, vmem),
        scratch_shapes=[pltpu.SMEM((replicas,), jnp.int32)],
        compiler_params=pltpu.CompilerParams(vmem_limit_bytes=VMEM_LIMIT),
        name="pack",
    )(sender, target, history, fill, switch, tiles, table, unfinished, fresh)


def partial(query, keys, values, bias):
    scores = head_scores(query, keys, bias)
    best = jnp.max(scores, axis=-1, keepdims=True)
    probs = jnp.exp2(scores - best)
    total = jnp.sum(probs, axis=-1, keepdims=True)
    return jnp.dot(probs.astype(jnp.bfloat16), values, preferred_element_type=jnp.float32), best, total


def diagonal(size):
    return lax.broadcasted_iota(jnp.int32, (size, size), 0) == lax.broadcasted_iota(jnp.int32, (size, size), 1)


def attend_kernel(
    cap, plane, lines, total_width,
    query, count, bias, gain, tiles, tails, outgoing,
    out,
    arrived, asked, asked_count, answer, answer_log, given, given_log, mixed, top, total, attn, square,
    own_sem, tile_send, tile_recv, ask_send, ask_recv, count_send, count_recv,
    answer_send, answer_recv, log_send, log_recv, square_sem,
):
    steps, requests, heads, hdim = query.shape
    pool, _, kv, page, _ = tiles.shape
    group = heads // kv
    groups = steps * requests
    rows = groups * group
    tokens = plane * cap * page
    me = lax.axis_index("rep")
    core = lax.axis_index("tp")
    line, place = lax.div(me, plane), lax.rem(me, plane)

    def peer(a_line, a_place):
        return {"rep": a_line * plane + a_place}

    def send(source, target, send_sem, recv_sem, device):
        return pltpu.make_async_remote_copy(
            src_ref=source, dst_ref=target, send_sem=send_sem, recv_sem=recv_sem,
            device_id=device, device_id_type=pl.DeviceIdType.MESH,
        )

    def line_at(step):
        return lax.rem(line + step, lines)

    def line_back(step):
        return lax.rem(line + lines - step, lines)

    def place_at(step):
        if plane == 4:
            if step in (1, 2):
                step = step + core * (3 - 2 * step)
            y, x = lax.div(place, 2), lax.rem(place, 2)
            return lax.rem(y + step // 2, 2) * 2 + lax.rem(x + step % 2, 2)
        return lax.rem(place + step, plane)

    barrier = pltpu.get_barrier_semaphore()
    for j in range(1, lines):
        pl.semaphore_signal(barrier, inc=1, device_id=peer(line_at(j), place), device_id_type=pl.DeviceIdType.MESH)
    for i in range(1, plane):
        pl.semaphore_signal(barrier, inc=1, device_id=peer(line, place_at(i)), device_id_type=pl.DeviceIdType.MESH)
    pl.semaphore_signal(barrier, inc=1, device_id={"tp": 1 - core}, device_id_type=pl.DeviceIdType.MESH)
    pl.semaphore_wait(barrier, lines + plane - 1)

    def ask(j):
        to = line_at(j)
        return (
            send(query, asked.at[line], ask_send.at[to], ask_recv.at[line], peer(to, place)),
            send(count.at[to], asked_count.at[line], count_send.at[to], count_recv.at[line], peer(to, place)),
        )

    def ship(j, i):
        to = line_at(j)
        mate = place_at(i)
        return send(
            outgoing.at[to * plane + mate], arrived.at[to, place],
            tile_send.at[to, mate], tile_recv.at[to, place], peer(line, mate),
        )

    def keep(j):
        to = line_at(j)
        return pltpu.make_async_copy(outgoing.at[to * plane + place], arrived.at[to, place], own_sem.at[to])

    def reply(j):
        to = line_at(j)
        return (
            send(answer.at[to], given.at[line], answer_send.at[to], answer_recv.at[line], peer(to, place)),
            send(answer_log.at[to], given_log.at[line], log_send.at[to], log_recv.at[line], peer(to, place)),
        )

    for j in range(1, lines + 1):
        for i in range(1, plane):
            ship(j, i).start()
        keep(j).start()
        if j < lines:
            for copy in ask(lines - j):
                copy.start()

    def pool_head(k, carry):
        q = query[:, :, pl.ds(k * group, group), :].reshape(rows, hdim)
        both = [
            jnp.concatenate(
                [tiles[:, c, k].reshape(pool * page, hdim), tails[:, c, k].reshape(requests * page, hdim)], 0
            )
            for c in range(2)
        ]
        mixed[k], top[k], total[k] = partial(q, both[0], both[1], bias[...])
        return carry

    lax.fori_loop(0, kv, pool_head, 0)

    width = cap * page
    repeat = (
        lax.broadcasted_iota(jnp.int32, (hdim, tokens), 1) % width
        == lax.broadcasted_iota(jnp.int32, (hdim, tokens), 0)
    )
    repeat = jnp.where(repeat, 1.0, 0.0).astype(jnp.bfloat16)
    mine = (
        lax.broadcasted_iota(jnp.int32, (plane, tokens), 1) // width
        == lax.broadcasted_iota(jnp.int32, (plane, tokens), 0)
    )
    eye = diagonal(rows)

    def filled(to):
        here = arrived[to, :, 2 * kv * cap, 0, :]
        spread = jnp.dot(here, repeat, preferred_element_type=jnp.float32)
        return jnp.sum(jnp.where(mine, spread, 0.0), axis=0, keepdims=True)

    def arrivals(to, k):
        keys = arrived[to, :, pl.ds(k * cap, cap)].reshape(tokens, hdim)
        values = arrived[to, :, pl.ds((kv + k) * cap, cap)].reshape(tokens, hdim)
        return keys, values

    for j in range(1, lines):
        to = line_at(j)
        for i in range(1, plane):
            source = place_at(i)
            send(
                outgoing.at[0], arrived.at[to, source], tile_send.at[to, source], tile_recv.at[to, source],
                peer(line, source),
            ).wait_recv()
        keep(j).wait()
        send(query, asked.at[to], ask_send.at[to], ask_recv.at[to], peer(to, place)).wait_recv()
        send(
            count.at[to], asked_count.at[to], count_send.at[to], count_recv.at[to], peer(to, place)
        ).wait_recv()
        set_bias = bias_of(asked_count[to].astype(jnp.float32) * filled(to))

        def set_head(k, carry):
            q = asked[to, :, :, pl.ds(k * group, group), :].reshape(rows, hdim)
            keys, values = arrivals(to, k)
            part, best, amount = partial(q, keys, values, set_bias)
            answer[to, k] = (part / amount).astype(jnp.bfloat16)
            log = best + jnp.log2(amount)
            answer_log[to, k] = jnp.sum(jnp.where(eye, log, 0.0), axis=0, keepdims=True)
            return carry

        lax.fori_loop(0, kv, set_head, 0)
        for copy in reply(j):
            copy.start()

    for i in range(1, plane):
        source = place_at(i)
        send(
            outgoing.at[0], arrived.at[line, source], tile_send.at[line, source], tile_recv.at[line, source],
            peer(line, source),
        ).wait_recv()
    keep(lines).wait()
    last_bias = bias_of(count[line].astype(jnp.float32) * filled(line))

    def last_head(k, carry):
        q = query[:, :, pl.ds(k * group, group), :].reshape(rows, hdim)
        keys, values = arrivals(line, k)
        part, best, amount = partial(q, keys, values, last_bias)
        high = jnp.maximum(best, top[k])
        fresh, old = jnp.exp2(best - high), jnp.exp2(top[k] - high)
        mixed[k] = part * fresh + mixed[k] * old
        total[k] = amount * fresh + total[k] * old
        top[k] = high
        return carry

    lax.fori_loop(0, kv, last_head, 0)

    for j in range(1, lines):
        to = line_at(j)
        send(answer.at[to], given.at[to], answer_send.at[to], answer_recv.at[to], peer(to, place)).wait_recv()
        send(answer_log.at[to], given_log.at[to], log_send.at[to], log_recv.at[to], peer(to, place)).wait_recv()

    square[0] = jnp.zeros_like(square[0])

    def merge_head(k, carry):
        logs = []
        high = top[k]
        for j in range(1, lines):
            log = jnp.sum(jnp.where(eye, given_log[line_at(j), k], 0.0), axis=1, keepdims=True)
            logs.append(log)
            high = jnp.maximum(high, log)
        old = jnp.exp2(top[k] - high)
        whole = mixed[k] * old
        amount = total[k] * old
        for j in range(1, lines):
            share = jnp.exp2(logs[j - 1] - high)
            whole = whole + given[line_at(j), k].astype(jnp.float32) * share
            amount = amount + share
        result = (whole / amount).astype(jnp.bfloat16)
        attn[:, :, pl.ds(k * group, group), :] = result.reshape(steps, requests, group, hdim)
        wide = result.astype(jnp.float32)
        square[0] += jnp.sum((wide * wide).reshape(groups, group, hdim), axis=1)
        return carry

    lax.fori_loop(0, kv, merge_head, 0)
    swap = send(square.at[0], square.at[1], square_sem.at[0], square_sem.at[1], {"tp": 1 - core})
    swap.start()
    swap.wait()
    mean = jnp.sum(square[0] + square[1], axis=-1, keepdims=True) / total_width
    scale = lax.rsqrt(mean + 1e-05)
    for t in range(steps):
        for g in range(requests):
            row = t * requests + g
            wide = attn[t, g].astype(jnp.float32)
            out[t, g] = (wide * scale[row : row + 1, :] * gain[...]).astype(out.dtype)

    for j in range(1, lines + 1):
        for i in range(1, plane):
            ship(j, i).wait_send()
        if j < lines:
            for copy in ask(j) + reply(j):
                copy.wait_send()


def attend(query, count, bias, gain, tiles, tails, outgoing, cap, plane):
    steps, requests, heads, hdim = query.shape
    kv, page = tiles.shape[2:4]
    lines = outgoing.shape[0] // plane
    rows = steps * requests * heads // kv
    vmem = pl.BlockSpec(memory_space=pltpu.VMEM)
    dma = pltpu.SemaphoreType.DMA
    return pl.pallas_call(
        functools.partial(attend_kernel, cap, plane, lines, heads * hdim * lax.axis_size("tp")),
        out_shape=jax.ShapeDtypeStruct(query.shape, jnp.bfloat16),
        in_specs=[vmem] * 6 + [pl.BlockSpec(memory_space=pl.ANY)],
        out_specs=vmem,
        scratch_shapes=[
            pltpu.VMEM((lines, plane) + outgoing.shape[1:], jnp.bfloat16),
            pltpu.VMEM((lines,) + query.shape, jnp.bfloat16),
            pltpu.VMEM(count.shape, jnp.bfloat16),
            pltpu.VMEM((lines, kv, rows, hdim), jnp.bfloat16),
            pltpu.VMEM((lines, kv, 1, rows), jnp.float32),
            pltpu.VMEM((lines, kv, rows, hdim), jnp.bfloat16),
            pltpu.VMEM((lines, kv, 1, rows), jnp.float32),
            pltpu.VMEM((kv, rows, hdim), jnp.float32),
            pltpu.VMEM((kv, rows, 1), jnp.float32),
            pltpu.VMEM((kv, rows, 1), jnp.float32),
            pltpu.VMEM(query.shape, jnp.bfloat16),
            pltpu.VMEM((2, steps * requests, hdim), jnp.float32),
            dma((lines,)),
            dma((lines, plane)),
            dma((lines, plane)),
        ]
        + [dma((lines,))] * 8
        + [dma((2,))],
        compiler_params=pltpu.CompilerParams(
            vmem_limit_bytes=VMEM_LIMIT, collective_id=0, has_side_effects=True
        ),
        name="attend",
    )(query, count, bias, gain, tiles, tails, outgoing)


def body(query, fresh, unfinished, store, table, history, fill, sender, target, switch, gain):
    replicas = lax.axis_size("rep")
    steps, requests, heads, hdim = query.shape
    cap = max(2, 2 * sender.shape[0] // replicas)
    plane = math.gcd(4, replicas)
    tiles = jnp.transpose(store, (0, 1, 3, 2, 4))
    outgoing, count, bias, tails = pack(
        tiles, sender, target.reshape(-1), table, history, fill, switch,
        jnp.transpose(unfinished, (0, 1, 3, 2, 4)), fresh, replicas, cap, plane,
    )
    normed = attend(query, count, bias, gain.reshape(heads, hdim), tiles, tails, outgoing, cap, plane)
    return normed.reshape(steps, requests, heads * hdim)


def solution(mesh):
    placed = (
        P(None, "rep", "tp", None),
        P(None, "rep", None, "tp", None),
        P("rep", None, None, "tp", None),
        P("rep", None, None, "tp", None),
        P("rep", None),
        P("rep"),
        P("rep"),
        P("rep"),
        P("rep", None),
        P("rep"),
        P("tp"),
    )
    return jax.shard_map(
        body, mesh=mesh, in_specs=placed, out_specs=P(None, "rep", "tp"), check_vma=False
    )
```
